768 devices in a mesh: dp: 16 (over y, core), seq: 4 (over x), pool: 12 (over z).
Axes of the slice: x: 4, y: 8, z: 12, core: 2. Of those that a mesh axis runs over, the one named last changes fastest.
Arguments:
- events: bfloat16 [98304, 1024], P(('dp', 'seq', 'pool')), may hold values from -6 to 6
- input_weight: bfloat16 [1024, 4096], replicated, may hold values from -0.1875 to 0.1875
- output_weight: bfloat16 [1024, 1024], replicated, may hold values from -0.1875 to 0.1875
- positives: bfloat16 [98304, 1024], P(('dp', 'seq', 'pool')), may hold values from -8 to 8
- negatives: bfloat16 [1536, 1024], P('pool'), may hold values from -6 to 6
- log_probs: bfloat16 [1536], P('pool'), may hold values from -15 to -4
- lengths: int32 [768], replicated, may hold values from 1 to 256, 98304 in all
Outputs:
- d_events: float32 [98304, 1024], P(('dp', 'seq', 'pool'))
- d_output_weight: float32 [1024, 1024], P(('dp', 'seq'))
The draws below stay inside these ranges and needn't reach their ends.
Inputs may be any that keep to these rules, and one draw needn't show every extreme that they name: The histories lie end to end over all 98304 events, their lengths sum to 98304, and one history has exactly 256 events.
All inputs are finite; a program needn't handle non-finite values.
Results may differ from the reference program's by a relative error of at most 0.0095.
Values may be sent and summed in bfloat16 or wider, within the bound.
A program may use at most 64 MiB of HBM per device.

```python
import math
import jax
import jax.numpy as jnp
import numpy as np
from jax import lax

D = 1024
HEADS = 8
EV_DEV = 128
REACH = 2
NEG_DEV = 128
LONGEST = 256
EVENTS = 98304
NEG = 1536
USERS = 768


def event_rows_common(key):
    base_key = jax.random.fold_in(key, 7101)
    return jnp.clip(jax.random.normal(base_key, (EVENTS, D), jnp.float32), -6.0, 6.0)


def draw_events(key, part):
    return event_rows_common(key).astype(jnp.bfloat16)


def draw_positives(key, part):
    base_rows = event_rows_common(key)
    noise_rows = jnp.clip(jax.random.normal(jax.random.fold_in(key, 7202), (EVENTS, D), jnp.float32), -4.0, 4.0)
    top_share = 1.0
    mix_share = jax.random.uniform(jax.random.fold_in(key, 7203), (EVENTS, 1), jnp.float32, 0.0, top_share)
    return jnp.clip(base_rows + mix_share * noise_rows, -8.0, 8.0).astype(jnp.bfloat16)


def draw_log_probs(key, part):
    pool_count = NEG // NEG_DEV
    shard_span = max(pool_count - 1, 1)
    shard_index = (jnp.arange(NEG, dtype=jnp.int32) // NEG_DEV).astype(jnp.float32)
    rise_span = math.log(3.0)
    jitter = jax.random.uniform(jax.random.fold_in(key, 7301), (NEG,), jnp.float32, -1.0, 1.0)
    neg_log = 14.5 - math.log(NEG) + rise_span * shard_index / shard_span + jitter
    return (-neg_log).astype(jnp.bfloat16)


def steps_of(key, dims, cuts, low, high):
    gain = 1.0
    for dim, parts in cuts:
        steps = jax.random.uniform(jax.random.fold_in(jax.random.fold_in(key, 6), dim), (parts,), jnp.float32, low / len(cuts), high / len(cuts))
        gain = gain * jnp.repeat(jnp.exp(steps), dims[dim] // parts).reshape((-1,) + (1,) * (len(dims) - 1 - dim))
    return gain


def split_up(count, total, reach, skew):
    weights = [(1 << 20) // math.isqrt(grade ** skew) + 1 for grade in range(2, count + 1)]
    surplus, holding = total - reach - (count - 1), [1] * (count - 1)
    while surplus > 0:
        movable = [i for i in range(count - 1) if holding[i] < reach]
        mass, budget = sum([weights[i] for i in movable]), surplus
        for i in movable:
            more = min(reach - holding[i], max(1, budget * weights[i] // mass), surplus)
            holding[i] = holding[i] + more
            surplus = surplus - more
    return np.array([reach] + holding)


def ragged_sizes(stream_key, amount, total, bound, slope):
    if amount == 2:
        one = jax.random.randint(stream_key, (), max(1, total - bound), min(bound, total - 1) + 1)
        return jnp.stack([one, total - one])
    sizes = jnp.asarray(split_up(amount, total, bound, slope), jnp.int32)
    twos = (amount - 1) // 2
    giver, sink = sizes[1:1 + 2 * twos:2], sizes[2:2 + 2 * twos:2]
    room = jnp.minimum(giver - 1, bound - sink)
    passed = jax.random.randint(jax.random.fold_in(stream_key, 1), (twos,), 0, 1 << 20) % (room + 1)
    sizes = sizes.at[1:1 + 2 * twos:2].set(giver - passed).at[2:2 + 2 * twos:2].set(sink + passed)
    return sizes[jax.random.permutation(jax.random.fold_in(stream_key, 2), amount)]


def normal_values(own_key, dims, deviation, bound, split=(), kind=jnp.bfloat16):
    values = deviation * jax.random.normal(own_key, dims, jnp.float32)
    if split:
        values = values * steps_of(own_key, dims, split, -0.22, 0.18)
    return jnp.clip(values, -bound, bound).astype(kind)


def setup_inputs(seed: int = 0) -> dict:
    arg_keys = jax.random.split(jax.random.key(seed), 8)
    return {
        "events": draw_events(jax.random.fold_in(arg_keys[7], 71), 0),
        "input_weight": normal_values(arg_keys[1], (D, 4 * D), D ** -0.5, 0.1875),
        "output_weight": normal_values(arg_keys[2], (D, D), D ** -0.5, 0.1875),
        "positives": draw_positives(jax.random.fold_in(arg_keys[7], 71), 0),
        "negatives": normal_values(arg_keys[4], (NEG, D), 1.0, 6.0, ((0, 12),)),
        "log_probs": draw_log_probs(jax.random.fold_in(arg_keys[7], 71), 0),
        "lengths": ragged_sizes(arg_keys[6], USERS, EVENTS, LONGEST, 2).astype(jnp.int32),
    }


epsilon = 1e-05
sharpness_divisor = 0.05
loss_multiplier = 8.0

def normalize(row_data):
    centred = row_data - lax.optimization_barrier(jnp.mean(row_data, axis=1, keepdims=True))
    inv_std = lax.rsqrt(lax.optimization_barrier(jnp.mean(centred * centred, axis=1, keepdims=True)) + epsilon)
    return (centred * inv_std, inv_std)

def norm_back(grad_in, normed, inv_std):
    return (grad_in - lax.optimization_barrier(jnp.mean(grad_in, axis=1, keepdims=True)) - normed * lax.optimization_barrier(jnp.mean(grad_in * normed, axis=1, keepdims=True))) * inv_std

def silu_slope(values):
    sigmoid_v = jax.nn.sigmoid(values)
    return sigmoid_v * (1.0 + values * (1.0 - sigmoid_v))

def history_starts(lengths, first_row, row_count):
    starts = (jnp.cumsum(lengths) - lengths).astype(jnp.int32)
    positions = (first_row + jnp.arange(row_count, dtype=jnp.int32)).astype(jnp.int32)
    owner_start = lax.optimization_barrier(jnp.max(jnp.where(starts[None, :] <= positions[:, None], starts[None, :], 0), axis=1))
    return (owner_start, positions)

def visible(owner_start, positions, key_rows):
    allowed = (key_rows[None, :] >= owner_start[:, None]) & (key_rows[None, :] <= positions[:, None])
    return allowed.astype(jnp.float32)

def reference(events, input_weight, output_weight, positives, negatives, log_probs, lengths):
    feature_width = D
    row_count = EV_DEV
    reach_count = REACH
    block_count = EVENTS // EV_DEV
    head_size = feature_width // HEADS
    key_scale = 1.0 / math.sqrt(head_size)
    earlier_count = reach_count * row_count
    key_count = earlier_count + row_count
    event_blocks = events.reshape(block_count, row_count, feature_width)
    positive_blocks = positives.reshape(block_count, row_count, feature_width)
    negative_rows = negatives.astype(jnp.float32)
    sampled_decoy_vectors = (negative_rows * lax.rsqrt(lax.optimization_barrier(jnp.sum(negative_rows * negative_rows, axis=1, keepdims=True)))).astype(jnp.bfloat16)
    sequence_boundary_indices = log_probs.astype(jnp.float32)

    def project(block_idx):
        safe_idx = jnp.maximum(block_idx, 0).astype(jnp.int32)
        event_rows = lax.dynamic_index_in_dim(event_blocks, safe_idx, 0, keepdims=False).astype(jnp.float32)
        normed, inv_std = normalize(event_rows)
        return jnp.dot(normed.astype(jnp.bfloat16), input_weight, preferred_element_type=jnp.float32)

    def scan_step(state_in, block_idx):
        pre_stack, pending, weight_sum = state_in
        pre_act = pre_stack[0]
        event_rows = lax.dynamic_index_in_dim(event_blocks, block_idx, 0, keepdims=False).astype(jnp.float32)
        normed_x, inv_x = normalize(event_rows)
        oldest = project(block_idx - reach_count)
        prior_pres = jnp.concatenate([pre_stack[1:], oldest[None]], axis=0)
        prior_kv = jax.nn.silu(prior_pres[::-1]).astype(jnp.bfloat16)[:, :, 2 * feature_width:].reshape(earlier_count, 2 * feature_width)
        activated = jax.nn.silu(pre_act).astype(jnp.bfloat16)
        update_rows = activated[:, :feature_width]
        queries = activated[:, feature_width:2 * feature_width]
        key_values = activated[:, 2 * feature_width:]
        kv_all = jnp.concatenate([prior_kv, key_values], axis=0)
        keys_all = kv_all[:, :feature_width]
        values_all = kv_all[:, feature_width:]
        first_row = (block_idx * row_count).astype(jnp.int32)
        owner_start, positions = history_starts(lengths, first_row, row_count)
        key_rows = (first_row - earlier_count + jnp.arange(key_count, dtype=jnp.int32)).astype(jnp.int32)
        allowed = visible(owner_start, positions, key_rows)
        query_heads = queries.astype(jnp.float32).reshape(row_count, HEADS, head_size)
        key_heads = keys_all.astype(jnp.float32).reshape(key_count, HEADS, head_size)
        value_heads = values_all.astype(jnp.float32).reshape(key_count, HEADS, head_size)
        scores = jnp.einsum('ihd,jhd->hij', query_heads, key_heads) * key_scale
        weights = (jax.nn.silu(scores) * allowed[None] / EV_DEV).astype(jnp.bfloat16)
        mixed_out = jnp.einsum('hij,jhd->ihd', weights.astype(jnp.float32), value_heads).reshape(row_count, feature_width)
        normed_o, inv_o = normalize(mixed_out)
        update32 = update_rows.astype(jnp.float32)
        gated_rows = (normed_o * update32).astype(jnp.bfloat16)
        layer_out = jnp.dot(gated_rows, output_weight, preferred_element_type=jnp.float32) + event_rows
        inv_norm = lax.rsqrt(lax.optimization_barrier(jnp.sum(layer_out * layer_out, axis=1, keepdims=True)))
        normalized_result_vector = layer_out * inv_norm
        positive_rows = lax.dynamic_index_in_dim(positive_blocks, block_idx, 0, keepdims=False).astype(jnp.float32)
        target_normalized_vectors = positive_rows * lax.rsqrt(lax.optimization_barrier(jnp.sum(positive_rows * positive_rows, axis=1, keepdims=True)))
        target_similarity = lax.optimization_barrier(jnp.sum(normalized_result_vector * target_normalized_vectors, axis=1)) / sharpness_divisor
        similarity_values_matrix = jnp.dot(normalized_result_vector.astype(jnp.bfloat16), sampled_decoy_vectors.T, preferred_element_type=jnp.float32) / sharpness_divisor - sequence_boundary_indices[None, :]
        exp_terms = jnp.exp(similarity_values_matrix)
        target_exp_term = jnp.exp(target_similarity)
        partition_denominator = target_exp_term + lax.optimization_barrier(jnp.sum(exp_terms, axis=1))
        probability_mixed_vectors = jnp.dot(exp_terms.astype(jnp.bfloat16), sampled_decoy_vectors, preferred_element_type=jnp.float32)
        derivative_normalized_matrix = loss_multiplier / sharpness_divisor * (probability_mixed_vectors / partition_denominator[:, None] + (target_exp_term / partition_denominator - 1.0)[:, None] * target_normalized_vectors)
        grad_out = (derivative_normalized_matrix - normalized_result_vector * lax.optimization_barrier(jnp.sum(normalized_result_vector * derivative_normalized_matrix, axis=1, keepdims=True))) * inv_norm
        grad_low = grad_out.astype(jnp.bfloat16)
        weight_term = jnp.dot(gated_rows.T, grad_low, preferred_element_type=jnp.float32)
        grad_gated = jnp.dot(grad_low, output_weight.T, preferred_element_type=jnp.float32)
        grad_update = grad_gated * normed_o
        grad_normed = grad_gated * update32
        grad_mixed = norm_back(grad_normed, normed_o, inv_o).astype(jnp.bfloat16)
        grad_heads = grad_mixed.astype(jnp.float32).reshape(row_count, HEADS, head_size)
        grad_values = jnp.einsum('hij,ihd->jhd', weights.astype(jnp.float32), grad_heads).reshape(key_count, feature_width)
        grad_weights = jnp.einsum('ihd,jhd->hij', grad_heads, value_heads)
        grad_scores = (grad_weights * allowed[None] / EV_DEV * silu_slope(scores)).astype(jnp.bfloat16)
        grad_scores32 = grad_scores.astype(jnp.float32)
        grad_query = jnp.einsum('hij,jhd->ihd', grad_scores32, key_heads).reshape(row_count, feature_width) * key_scale
        grad_keys = jnp.einsum('hij,ihd->jhd', grad_scores32, query_heads).reshape(key_count, feature_width) * key_scale
        grad_kv = jnp.concatenate([grad_keys, grad_values], axis=1).reshape(reach_count + 1, row_count, 2 * feature_width)
        own_kv = grad_kv[reach_count] + pending[0]
        carried = jnp.concatenate([pending[1:], jnp.zeros((1, row_count, 2 * feature_width), jnp.float32)], axis=0)
        new_pending = carried + grad_kv[:reach_count][::-1]
        grad_act = jnp.concatenate([grad_update, grad_query, own_kv], axis=1)
        grad_pre = (grad_act * silu_slope(pre_act)).astype(jnp.bfloat16)
        grad_x = jnp.dot(grad_pre, input_weight.T, preferred_element_type=jnp.float32)
        grad_block = norm_back(grad_x, normed_x, inv_x) + grad_out
        return ((prior_pres, new_pending, weight_sum + weight_term), grad_block)
    start_stack = jnp.stack([project(jnp.int32(block_count - 1 - back_index)) for back_index in range(reach_count)], axis=0)
    initial = (start_stack, jnp.zeros((reach_count, row_count, 2 * feature_width), jnp.float32), jnp.zeros((feature_width, feature_width), jnp.float32))
    final_state, grad_blocks = lax.scan(scan_step, initial, jnp.arange(block_count, dtype=jnp.int32), reverse=True)
    return (grad_blocks.reshape(EVENTS, feature_width), final_state[2])
```

```python
import functools
import math

import jax
import jax.numpy as jnp
from jax import lax
from jax.experimental import pallas as pl
from jax.experimental.pallas import tpu as pltpu
from jax.sharding import PartitionSpec as P

HEADS = 8
EV_DEV = 128

epsilon = 1e-05
sharpness_divisor = 0.05
loss_multiplier = 8.0

MESH = pl.DeviceIdType.MESH
AXES = ("dp", "seq", "pool")
NT = (((1,), (1,)), ((), ()))
NN = (((1,), (0,)), ((), ()))
HALVES = 2
F32 = jnp.float32
BF16 = jnp.bfloat16


def dot(a, b, dims=NN):
    return lax.dot_general(a, b, dims, preferred_element_type=F32)


def slope(v):
    sg = jax.nn.sigmoid(v)
    return sg * (1.0 + v * (1.0 - sg))


def mean_last(v):
    return jnp.mean(v, axis=1, keepdims=True)


def normalize(row_data):
    centred = row_data - mean_last(row_data)
    inv_std = lax.rsqrt(mean_last(centred * centred) + epsilon)
    return centred * inv_std, inv_std


def norm_back(grad_in, normed, inv_std):
    return (grad_in - mean_last(grad_in) - normed * mean_last(grad_in * normed)) * inv_std


def kernel(
    sizes,
    lens_ref,
    lp_ref,
    ev_hbm,
    win_hbm,
    wout_hbm,
    pos_hbm,
    neg_hbm,
    dev_hbm,
    dw_ref,
    ev,
    win,
    wout,
    pos,
    negs_raw,
    xn,
    normed_x,
    slopes,
    upd,
    qb,
    kb,
    vb,
    mask_f,
    mask_t,
    sc_slope,
    mixed,
    neg,
    lpb,
    ebuf,
    unit,
    gout,
    gl2,
    gt,
    gt_sib,
    gm,
    gact,
    gpre,
    dout,
    send_a,
    recv_x,
    own_b,
    send_b,
    recv_y,
    own_c,
    send_c,
    recv_z,
    fin,
    load_sem,
    halo_s,
    halo_r,
    gm_s,
    gm_r,
    ring_s,
    ring_r,
    xs_s,
    xs_r,
    sib_s,
    sib_r,
    lp_s,
    lp_r,
    pair_s,
    pair_r,
    dwx_s,
    dwx_r,
    dwy_s,
    dwy_r,
    dwz_s,
    dwz_r,
    fin_s,
    fin_r,
):
    ny, nx, nz, width, heads, events_all = sizes
    hw = width // heads
    rows = EV_DEV
    cb = 256
    ups, dns = nz // 2, nz - 1 - nz // 2
    reds = fin.shape[0]
    tw = fin.shape[2]
    out_rows = fin.shape[1]
    scale = 1.0 / math.sqrt(hw)

    dp = lax.axis_index("dp")
    sx = lax.axis_index("seq")
    pz = lax.axis_index("pool")
    core = lax.rem(dp, 2)
    yy = lax.div(dp, 2)
    other = dp + 1 - 2 * core
    total = 2 * ny * nx * nz
    me = (dp * nx + sx) * nz + pz

    def place(i):
        return (lax.div(i, nx * nz), lax.rem(lax.div(i, nz), nx), lax.rem(i, nz))

    nxt = place(lax.rem(me + 1, total))
    prv = place(lax.rem(me + total - 1, total))
    sib = (other, sx, pz)

    def at_x(d):
        return (dp, lax.rem(sx + d, nx), pz)

    def at_y(d):
        return (lax.rem(yy + d, ny) * 2 + core, sx, pz)

    def at_z(d):
        return (dp, sx, lax.rem(pz + d, nz))

    def load(i, src, dst):
        return pltpu.make_async_copy(src, dst, load_sem.at[i])

    def remote(src, dst, s, r, dev):
        return pltpu.make_async_remote_copy(
            src_ref=src, dst_ref=dst, send_sem=s, recv_sem=r, device_id=dev, device_id_type=MESH
        )

    loads = [
        load(0, neg_hbm, negs_raw),
        load(1, ev_hbm, ev),
        load(2, win_hbm.at[:, pl.ds(2 * width, width)], win.at[2]),
        load(3, win_hbm.at[:, pl.ds(3 * width, width)], win.at[3]),
        load(4, win_hbm.at[:, pl.ds(width, width)], win.at[1]),
        load(5, win_hbm.at[:, pl.ds(0, width)], win.at[0]),
        load(6, wout_hbm, wout),
        load(7, pos_hbm, pos),
    ]
    for item in loads:
        item.start()

    barrier = pltpu.get_barrier_semaphore()
    partners = [nxt, prv, sib]
    partners += [at_x(d) for d in range(1, nx)]
    partners += [at_y(d) for d in range(1, ny)]
    partners += [at_z(d) for d in range(1, nz)]
    for partner in partners:
        pl.semaphore_signal(barrier, inc=1, device_id=partner, device_id_type=MESH)

    half = rows // HALVES

    def halo(kind, p):
        a, b, dev = ((2, 1, nxt), (2, 3, prv), (1, 0, nxt), (3, 4, prv))[kind]
        part = pl.ds(p * half, half)
        return remote(
            xn.at[a, part], xn.at[b, part], halo_s.at[kind, p], halo_r.at[kind, p], dev
        )

    def gm_hop(kind, p):
        part = pl.ds(p * half, half)
        return remote(
            gm.at[kind, part], gm.at[kind + 1, part], gm_s.at[kind, p], gm_r.at[kind, p], prv
        )

    piece = core * nx + sx

    def shard_at(way, s):
        return lax.rem(pz - s + nz, nz) if way == 0 else lax.rem(pz + s, nz)

    def ring(way, s):
        ref = neg.at[shard_at(way, s), piece]
        return remote(
            ref, ref, ring_s.at[way, s], ring_r.at[way, s], at_z(1) if way == 0 else at_z(nz - 1)
        )

    def ring_arrived(way, s):
        ref = neg.at[shard_at(way, s + 1), piece]
        dev = at_z(1) if way == 0 else at_z(nz - 1)
        return remote(ref, ref, ring_s.at[way, s], ring_r.at[way, s], dev)

    def cross(way, s, d):
        ref = neg.at[shard_at(way, s + 1), piece]
        return remote(ref, ref, xs_s.at[way, s, d - 1], xs_r.at[way, s, d - 1], at_x(d))

    def cross_arrived(way, s, d):
        from_x = core * nx + lax.rem(sx - d + nx, nx)
        ref = neg.at[shard_at(way, s + 1), from_x]
        return remote(ref, ref, xs_s.at[way, s, d - 1], xs_r.at[way, s, d - 1], at_x(d))

    def sib_copy(way, s):
        ref = neg.at[shard_at(way, s + 1), pl.ds(core * nx, nx)]
        return remote(ref, ref, sib_s.at[way, s], sib_r.at[way, s], sib)

    def sib_arrived(way, s):
        ref = neg.at[shard_at(way, s + 1), pl.ds((1 - core) * nx, nx)]
        return remote(ref, ref, sib_s.at[way, s], sib_r.at[way, s], sib)

    def lp_copy(d):
        return remote(lpb.at[pz], lpb.at[pz], lp_s.at[d - 1], lp_r.at[d - 1], at_z(d))

    def lp_arrived(d):
        ref = lpb.at[lax.rem(pz - d + nz, nz)]
        return remote(ref, ref, lp_s.at[d - 1], lp_r.at[d - 1], at_z(d))

    loads[0].wait()
    raw = negs_raw[...].astype(F32)
    unit_neg = raw * lax.rsqrt(jnp.sum(raw * raw, axis=1, keepdims=True))
    neg[pz] = unit_neg.astype(BF16).reshape(neg.shape[1:])
    lpb[pz] = lp_ref[...]
    loads[1].wait()
    own_x, inv_x = normalize(ev[...].astype(F32))
    normed_x[...] = own_x
    xn[2] = own_x.astype(BF16)

    pl.semaphore_wait(barrier, len(partners))

    for p in range(HALVES):
        halo(0, p).start()
        halo(1, p).start()
    ring(0, 0).start()
    if dns:
        ring(1, 0).start()
    for d in range(1, nz):
        lp_copy(d).start()

    def serve(way, s):
        ring_arrived(way, s).wait_recv()
        if s + 1 < (ups, dns)[way]:
            ring(way, s + 1).start()
        for d in range(1, nx):
            cross(way, s, d).start()

    served = [0]

    def serve_next(count=1):
        for _ in range(count):
            s = served[0]
            for way in (0, 1):
                if s < (ups, dns)[way]:
                    serve(way, s)
            served[0] = s + 1

    def project_own(chunk, dst):
        def body(j, carry):
            cols = pl.ds(pl.multiple_of(j * cb, cb), cb)
            pre = dot(xn[2], win[chunk, :, cols])
            sg = jax.nn.sigmoid(pre)
            slopes[chunk, :, cols] = sg * (1.0 + pre * (1.0 - sg))
            dst[:, cols] = (pre * sg).astype(BF16)
            return carry

        lax.fori_loop(0, width // cb, body, 0)

    def project(slot, chunk, dst):
        def body(j, carry):
            cols = pl.ds(pl.multiple_of(j * cb, cb), cb)
            pre = dot(xn[slot], win[chunk, :, cols])
            dst[:, cols] = (pre * jax.nn.sigmoid(pre)).astype(BF16)
            return carry

        lax.fori_loop(0, width // cb, body, 0)

    loads[2].wait()
    project_own(2, kb.at[2])
    loads[3].wait()
    project_own(3, vb.at[2])

    for p in range(HALVES):
        halo(0, p).wait_recv()
        halo(2, p).start()
        halo(1, p).wait_recv()
        halo(3, p).start()
    serve_next()

    loads[4].wait()
    project_own(1, qb.at[0])
    loads[5].wait()
    project_own(0, upd)
    serve_next()

    users = lens_ref.shape[1]
    lens8 = lens_ref[...].astype(BF16)
    ri = lax.broadcasted_iota(jnp.int32, (users, users), 0)
    ci = lax.broadcasted_iota(jnp.int32, (users, users), 1)
    before_cols = (ri < ci).astype(F32).astype(BF16)
    before_rows = (ci < ri).astype(F32).astype(BF16)
    starts_row = dot(lens8, before_cols)[0:1, :]
    starts_col = dot(before_rows, lens8, NT)[:, 0:1]
    first = (me * rows).astype(F32)
    own_pos = first + lax.broadcasted_iota(jnp.int32, (rows, 1), 0).astype(F32)
    own_first = jnp.max(jnp.where(starts_row <= own_pos, starts_row, 0.0), axis=1, keepdims=True)
    key_pos = first - 2.0 * rows + lax.broadcasted_iota(jnp.int32, (rows, 3 * rows), 1).astype(F32)
    mask_f[...] = jnp.where((key_pos >= own_first) & (key_pos <= own_pos), 1.0 / EV_DEV, 0.0)
    row_pos = first + lax.broadcasted_iota(jnp.int32, (1, 3 * rows), 1).astype(F32)
    row_first = jnp.max(jnp.where(starts_col <= row_pos, starts_col, 0.0), axis=0, keepdims=True)
    row_first = jnp.where(row_pos < events_all, row_first, float(2 * events_all))
    mask_t[...] = jnp.where((own_pos >= row_first) & (own_pos <= row_pos), 1.0 / EV_DEV, 0.0)
    serve_next()

    project(1, 2, kb.at[1])
    project(1, 3, vb.at[1])
    serve_next()
    project(3, 1, qb.at[1])
    serve_next()
    for p in range(HALVES):
        halo(2, p).wait_recv()
    project(0, 2, kb.at[0])
    project(0, 3, vb.at[0])
    serve_next(max(ups - 5, 0))

    def head_forward(h, carry):
        cols = pl.ds(pl.multiple_of(h * hw, hw), hw)
        keys = kb[:, :, cols].reshape(3 * rows, hw)
        values = vb[:, :, cols].reshape(3 * rows, hw)
        s = dot(qb[0, :, cols], keys, NT) * scale
        sg = jax.nn.sigmoid(s)
        seen = mask_f[...]
        sc_slope[h] = seen * (sg * (1.0 + s * (1.0 - sg)))
        w = (s * sg * seen).astype(BF16)
        mixed[:, cols] = dot(w, values)
        return carry

    lax.fori_loop(0, heads, head_forward, 0)

    for way in (0, 1):
        for s in range((ups, dns)[way]):
            for d in range(1, nx):
                cross_arrived(way, s, d).wait_recv()
            sib_copy(way, s).start()

    normed_o, inv_o = normalize(mixed[...])
    mixed[...] = normed_o
    gated = normed_o * upd[...].astype(F32)
    gated_low = gated.astype(BF16)
    x_rows = ev[...].astype(F32)
    loads[6].wait()
    layer_out = dot(gated_low, wout[...]) + x_rows
    inv_norm = lax.rsqrt(jnp.sum(layer_out * layer_out, axis=1, keepdims=True))
    unit_out = layer_out * inv_norm
    unit[...] = unit_out
    unit_low = unit_out.astype(BF16)

    per_y = width // ny
    for j in range(ny):
        turned = gated[:, j * per_y : (j + 1) * per_y].T.astype(BF16)
        for c in range(2):
            for k in range(nx):
                r0 = (c * nx + k) * out_rows
                gt[c, k, j] = turned[r0 : r0 + out_rows]
    to_sib_g = remote(gt.at[1 - core], gt_sib, pair_s.at[0], pair_r.at[0], sib)
    to_sib_g.start()

    loads[7].wait()
    pos_rows = pos[...].astype(F32)
    pos_unit = pos_rows * lax.rsqrt(jnp.sum(pos_rows * pos_rows, axis=1, keepdims=True))
    pos_exp = jnp.exp(jnp.sum(unit_out * pos_unit, axis=1, keepdims=True) / sharpness_divisor)

    for d in range(1, nz):
        lp_arrived(d).wait_recv()
    for way in (0, 1):
        for s in range((ups, dns)[way]):
            sib_arrived(way, s).wait_recv()

    def logits(z, exp_total):
        negs = neg[z].reshape(rows, width)
        lg = dot(unit_low, negs, NT) * (1.0 / sharpness_divisor) - lpb[z, 0:1, :]
        e = jnp.exp(lg)
        ebuf[:, pl.ds(pl.multiple_of(z * rows, rows), rows)] = e.astype(BF16)
        return exp_total + jnp.sum(e, axis=1, keepdims=True)

    exp_total = lax.fori_loop(0, nz, logits, jnp.zeros((rows, 1), F32))
    denominator = pos_exp + exp_total
    mixed_negs = dot(ebuf[...], neg[...].reshape(nz * rows, width))
    unit_out = unit[...]
    grad_unit = (
        loss_multiplier
        / sharpness_divisor
        * (mixed_negs / denominator + (pos_exp / denominator - 1.0) * pos_unit)
    )
    grad_out = (
        grad_unit - unit_out * jnp.sum(unit_out * grad_unit, axis=1, keepdims=True)
    ) * inv_norm
    gout[...] = grad_out
    gl2[0] = grad_out.astype(BF16)
    to_sib_l = remote(gl2.at[0], gl2.at[1], pair_s.at[1], pair_r.at[1], sib)
    to_sib_l.start()

    def gate_back(j, carry):
        cols = pl.ds(pl.multiple_of(j * cb, cb), cb)
        gact[:, cols] = dot(gl2[0], wout[cols, :], NT)
        return carry

    lax.fori_loop(0, width // cb, gate_back, 0)
    grad_gated = gact[...]
    normed_o = mixed[...]
    gpre[:, 0:width] = (grad_gated * normed_o * slopes[0]).astype(BF16)
    gm[0] = norm_back(grad_gated * upd[...].astype(F32), normed_o, inv_o).astype(BF16)
    for p in range(HALVES):
        gm_hop(0, p).start()

    to_sib_g.wait_recv()
    to_sib_l.wait_recv()

    def weight_part(k):
        mine = gt[core, k].reshape(ny * out_rows, rows)
        theirs = gt_sib[k].reshape(ny * out_rows, rows)
        left = jnp.concatenate([mine, theirs], axis=1)
        return dot(left, gl2[...].reshape(2 * rows, width))

    def dwx(d):
        return remote(
            send_a.at[d - 1], recv_x.at[d - 1], dwx_s.at[d - 1], dwx_r.at[d - 1], at_x(d)
        )

    for d in range(1, nx):
        send_a[d - 1] = weight_part(lax.rem(sx + d, nx)).astype(BF16).reshape(send_a.shape[1:])
        dwx(d).start()
    own_b[...] = weight_part(sx).reshape(own_b.shape)

    def head_query(h, carry):
        cols = pl.ds(pl.multiple_of(h * hw, hw), hw)
        values = vb[:, :, cols].reshape(3 * rows, hw)
        keys = kb[:, :, cols].reshape(3 * rows, hw)
        gs = (dot(gm[0, :, cols], values, NT) * sc_slope[h]).astype(BF16)
        gq = dot(gs, keys) * scale
        at = pl.ds(pl.multiple_of(width + h * hw, hw), hw)
        gpre[:, at] = (gq * slopes[1, :, cols]).astype(BF16)
        return carry

    lax.fori_loop(0, heads, head_query, 0)

    for p in range(HALVES):
        gm_hop(0, p).wait_recv()
        gm_hop(1, p).start()

    for p in range(HALVES):
        halo(3, p).wait_recv()
    project(4, 1, qb.at[2])

    def dwy(d):
        return remote(
            send_b.at[lax.rem(yy + d, ny)], recv_y.at[d - 1], dwy_s.at[d - 1], dwy_r.at[d - 1], at_y(d)
        )

    for d in range(1, nx):
        dwx(d).wait_recv()
    summed = own_b[...]
    for d in range(1, nx):
        summed = summed + recv_x[d - 1].astype(F32)
    own_b[...] = summed
    send_b[...] = summed.astype(BF16)
    for d in range(1, ny):
        dwy(d).start()

    for p in range(HALVES):
        gm_hop(1, p).wait_recv()

    def head_keys(h, carry):
        cols = pl.ds(pl.multiple_of(h * hw, hw), hw)
        queries = qb[:, :, cols].reshape(3 * rows, hw)
        grads = gm[:, :, cols].reshape(3 * rows, hw)
        s = dot(kb[2, :, cols], queries, NT) * scale
        sg = jax.nn.sigmoid(s)
        seen = mask_t[...]
        w = (s * sg * seen).astype(BF16)
        gv = dot(w, grads)
        gs = (dot(vb[2, :, cols], grads, NT) * seen * (sg * (1.0 + s * (1.0 - sg)))).astype(BF16)
        gk = dot(gs, queries) * scale
        at = pl.ds(pl.multiple_of(2 * width + h * hw, hw), hw)
        gpre[:, at] = (gk * slopes[2, :, cols]).astype(BF16)
        at = pl.ds(pl.multiple_of(3 * width + h * hw, hw), hw)
        gpre[:, at] = (gv * slopes[3, :, cols]).astype(BF16)
        return carry

    lax.fori_loop(0, heads, head_keys, 0)

    def dwz(d):
        return remote(
            send_c.at[lax.rem(pz + d, nz)], recv_z.at[d - 1], dwz_s.at[d - 1], dwz_r.at[d - 1], at_z(d)
        )

    def dwz_arrived(d):
        return remote(send_c.at[0], recv_z.at[d - 1], dwz_s.at[d - 1], dwz_r.at[d - 1], at_z(d))

    def fin_copy(d):
        return remote(fin.at[pz], fin.at[pz], fin_s.at[d - 1], fin_r.at[d - 1], at_z(d))

    def fin_arrived(d):
        ref = fin.at[lax.rem(pz - d + nz, nz)]
        return remote(ref, ref, fin_s.at[d - 1], fin_r.at[d - 1], at_z(d))

    for d in range(1, ny):
        dwy(d).wait_recv()
    summed = own_b[yy]
    for d in range(1, ny):
        summed = summed + recv_y[d - 1].astype(F32)
    for t in range(reds):
        own_c[t] = summed[:, t * tw : (t + 1) * tw]
        send_c[t] = summed[:, t * tw : (t + 1) * tw].astype(BF16)
    for d in range(1, nz):

        @pl.when(lax.rem(pz + d, nz) < reds)
        def _(d=d):
            dwz(d).start()

    def x_back(j, carry):
        cols = pl.ds(pl.multiple_of(j * cb, cb), cb)
        part = dot(gpre[:, 0:width], win[0, cols, :], NT)
        for c in range(1, 4):
            part = part + dot(gpre[:, c * width : (c + 1) * width], win[c, cols, :], NT)
        gact[:, cols] = part
        return carry

    lax.fori_loop(0, width // cb, x_back, 0)

    @pl.when(pz < reds)
    def _():
        for d in range(1, nz):
            dwz_arrived(d).wait_recv()
        done = own_c[pz]
        for d in range(1, nz):
            done = done + recv_z[d - 1].astype(F32)
        fin[pz] = done
        for d in range(1, nz):
            fin_copy(d).start()

    dout[...] = norm_back(gact[...], normed_x[...], inv_x) + gout[...]
    out_copy = pltpu.make_async_copy(dout, dev_hbm, load_sem.at[8])
    out_copy.start()

    for d in range(1, nz):

        @pl.when(lax.rem(pz - d + nz, nz) < reds)
        def _(d=d):
            fin_arrived(d).wait_recv()

    for t in range(reds):
        dw_ref[:, t * tw : (t + 1) * tw] = fin[t]
    out_copy.wait()

    for p in range(HALVES):
        for kind in range(4):
            halo(kind, p).wait_send()
        for kind in range(2):
            gm_hop(kind, p).wait_send()
    for way in (0, 1):
        for s in range((ups, dns)[way]):
            ring(way, s).wait_send()
            for d in range(1, nx):
                cross(way, s, d).wait_send()
            sib_copy(way, s).wait_send()
    for d in range(1, nz):
        lp_copy(d).wait_send()
    to_sib_g.wait_send()
    to_sib_l.wait_send()
    for d in range(1, nx):
        dwx(d).wait_send()
    for d in range(1, ny):
        dwy(d).wait_send()
    for d in range(1, nz):

        @pl.when(lax.rem(pz + d, nz) < reds)
        def _(d=d):
            dwz(d).wait_send()

    @pl.when(pz < reds)
    def _():
        for d in range(1, nz):
            fin_copy(d).wait_send()


def shards(mesh_sizes, events, input_weight, output_weight, positives, negatives, log_probs, lengths):
    ndp, nx, nz = mesh_sizes
    ny = ndp // 2
    rows, width = events.shape
    heads = HEADS
    users = lengths.shape[0]
    ups = nz // 2
    reds = 8 if nz >= 8 else 2
    tw = width // reds
    out_rows = width // (ndp * nx)
    piece_rows = rows // (2 * nx)
    events_all = rows * ndp * nx * nz
    lens8 = jnp.broadcast_to(lengths.astype(F32)[None, :], (8, users))
    lp8 = jnp.broadcast_to(log_probs.astype(F32)[None, :], (8, rows))
    v = pltpu.VMEM
    dma = pltpu.SemaphoreType.DMA
    scratch = [
        v((rows, width), BF16),
        v((4, width, width), BF16),
        v((width, width), BF16),
        v((rows, width), BF16),
        v((rows, width), BF16),
        v((5, rows, width), BF16),
        v((rows, width), F32),
        v((4, rows, width), F32),
        v((rows, width), BF16),
        v((3, rows, width), BF16),
        v((3, rows, width), BF16),
        v((3, rows, width), BF16),
        v((rows, 3 * rows), F32),
        v((rows, 3 * rows), F32),
        v((heads, rows, 3 * rows), F32),
        v((rows, width), F32),
        v((nz, 2 * nx, piece_rows, width), BF16),
        v((nz, 8, rows), F32),
        v((rows, nz * rows), BF16),
        v((rows, width), F32),
        v((rows, width), F32),
        v((2, rows, width), BF16),
        v((2, nx, ny, out_rows, rows), BF16),
        v((nx, ny, out_rows, rows), BF16),
        v((3, rows, width), BF16),
        v((rows, width), F32),
        v((rows, 4 * width), BF16),
        v((rows, width), F32),
        v((nx - 1, ny, out_rows, width), BF16),
        v((nx - 1, ny, out_rows, width), BF16),
        v((ny, out_rows, width), F32),
        v((ny, out_rows, width), BF16),
        v((ny - 1, out_rows, width), BF16),
        v((reds, out_rows, tw), F32),
        v((reds, out_rows, tw), BF16),
        v((nz - 1, out_rows, tw), BF16),
        v((reds, out_rows, tw), F32),
        dma((9,)),
        dma((4, HALVES)),
        dma((4, HALVES)),
        dma((2, HALVES)),
        dma((2, HALVES)),
        dma((2, ups)),
        dma((2, ups)),
        dma((2, ups, nx - 1)),
        dma((2, ups, nx - 1)),
        dma((2, ups)),
        dma((2, ups)),
        dma((nz - 1,)),
        dma((nz - 1,)),
        dma((2,)),
        dma((2,)),
        dma((nx - 1,)),
        dma((nx - 1,)),
        dma((ny - 1,)),
        dma((ny - 1,)),
        dma((nz - 1,)),
        dma((nz - 1,)),
        dma((nz - 1,)),
        dma((nz - 1,)),
    ]
    hbm = pl.BlockSpec(memory_space=pl.ANY)
    vmem = pl.BlockSpec(memory_space=pltpu.VMEM)
    return pl.pallas_call(
        functools.partial(kernel, (ny, nx, nz, width, heads, events_all)),
        out_shape=(
            jax.ShapeDtypeStruct((rows, width), F32),
            jax.ShapeDtypeStruct((out_rows, width), F32),
        ),
        in_specs=[vmem, vmem, hbm, hbm, hbm, hbm, hbm],
        out_specs=(hbm, vmem),
        scratch_shapes=scratch,
        compiler_params=pltpu.CompilerParams(
            collective_id=0, has_side_effects=True, vmem_limit_bytes=56 * 1024 * 1024
        ),
    )(lens8, lp8, events, input_weight, output_weight, positives, negatives)


def solution(mesh):
    sizes = tuple(mesh.shape[a] for a in AXES)
    placed = (
        P(AXES, None),
        P(),
        P(),
        P(AXES, None),
        P("pool", None),
        P("pool"),
        P(),
    )
    return jax.shard_map(
        functools.partial(shards, sizes),
        mesh=mesh,
        in_specs=placed,
        out_specs=(P(AXES, None), P(("dp", "seq"), None)),
        check_vma=False,
    )
```

```python
import functools
import math

import jax
import jax.numpy as jnp
from jax import lax
from jax.experimental import pallas as pl
from jax.experimental.pallas import tpu as pltpu
from jax.sharding import PartitionSpec as P

HEADS = 8
EV_DEV = 128

epsilon = 1e-05
sharpness_divisor = 0.05
loss_multiplier = 8.0

MESH = pl.DeviceIdType.MESH
AXES = ("dp", "seq", "pool")
NT = (((1,), (1,)), ((), ()))
NN = (((1,), (0,)), ((), ()))
HALVES = 2
F32 = jnp.float32
BF16 = jnp.bfloat16


def dot(a, b, dims=NN):
    return lax.dot_general(a, b, dims, preferred_element_type=F32)


def slope(v):
    sg = jax.nn.sigmoid(v)
    return sg * (1.0 + v * (1.0 - sg))


def mean_last(v):
    return jnp.mean(v, axis=1, keepdims=True)


def normalize(row_data):
    centred = row_data - mean_last(row_data)
    inv_std = lax.rsqrt(mean_last(centred * centred) + epsilon)
    return centred * inv_std, inv_std


def norm_back(grad_in, normed, inv_std):
    return (grad_in - mean_last(grad_in) - normed * mean_last(grad_in * normed)) * inv_std


def kernel(
    sizes,
    lens_ref,
    lp_ref,
    ev_hbm,
    win_hbm,
    wout_hbm,
    pos_hbm,
    neg_hbm,
    dev_hbm,
    dw_ref,
    ev,
    win,
    wout,
    pos,
    negs_raw,
    xn,
    normed_x,
    slopes,
    upd,
    qb,
    kb,
    vb,
    mask_f,
    mask_t,
    sc_slope,
    mixed,
    neg,
    lpb,
    ebuf,
    unit,
    gout,
    gl2,
    gt,
    gt_sib,
    gm,
    gact,
    gpre,
    dout,
    gkeys,
    gvals,
    send_a,
    recv_x,
    send_a2,
    recv_x2,
    part_x,
    own_b,
    send_b,
    recv_y,
    own_c,
    send_c,
    recv_z,
    fin,
    load_sem,
    halo_s,
    halo_r,
    gm_s,
    gm_r,
    ring_s,
    ring_r,
    xs_s,
    xs_r,
    sib_s,
    sib_r,
    lp_s,
    lp_r,
    pair_s,
    pair_r,
    dwx_s,
    dwx_r,
    dwy_s,
    dwy_r,
    dwz_s,
    dwz_r,
    fin_s,
    fin_r,
):
    ny, nx, nz, width, heads, events_all = sizes
    hw = width // heads
    rows = EV_DEV
    cb = 256
    ups, dns = nz // 2, nz - 1 - nz // 2
    reds = fin.shape[0]
    tw = fin.shape[2]
    out_rows = fin.shape[1]
    scale = 1.0 / math.sqrt(hw)

    dp = lax.axis_index("dp")
    sx = lax.axis_index("seq")
    pz = lax.axis_index("pool")
    core = lax.rem(dp, 2)
    yy = lax.div(dp, 2)
    other = dp + 1 - 2 * core
    total = 2 * ny * nx * nz
    me = (dp * nx + sx) * nz + pz

    def place(i):
        return (lax.div(i, nx * nz), lax.rem(lax.div(i, nz), nx), lax.rem(i, nz))

    nxt = place(lax.rem(me + 1, total))
    prv = place(lax.rem(me + total - 1, total))
    sib = (other, sx, pz)

    xa = sx + 1 - 2 * lax.rem(sx, 2)
    xb = nx - 1 - sx
    dev_a = (dp, xa, pz)
    dev_b = (dp, xb, pz)

    def at_y(d):
        return (lax.rem(yy + d, ny) * 2 + core, sx, pz)

    def at_z(d):
        return (dp, sx, lax.rem(pz + d, nz))

    def load(i, src, dst):
        return pltpu.make_async_copy(src, dst, load_sem.at[i])

    def remote(src, dst, s, r, dev):
        return pltpu.make_async_remote_copy(
            src_ref=src, dst_ref=dst, send_sem=s, recv_sem=r, device_id=dev, device_id_type=MESH
        )

    loads = [
        load(0, neg_hbm, negs_raw),
        load(1, ev_hbm, ev),
        load(2, win_hbm.at[:, pl.ds(2 * width, width)], win.at[2]),
        load(3, win_hbm.at[:, pl.ds(3 * width, width)], win.at[3]),
        load(4, win_hbm.at[:, pl.ds(width, width)], win.at[1]),
        load(5, win_hbm.at[:, pl.ds(0, width)], win.at[0]),
        load(6, wout_hbm, wout),
        load(7, pos_hbm, pos),
    ]
    for item in loads:
        item.start()

    barrier = pltpu.get_barrier_semaphore()
    partners = [nxt, prv, sib]
    partners += [dev_a, dev_b]
    partners += [at_y(d) for d in range(1, ny)]
    partners += [at_z(d) for d in range(1, nz)]
    for partner in partners:
        pl.semaphore_signal(barrier, inc=1, device_id=partner, device_id_type=MESH)

    half = rows // HALVES

    def halo(kind, p):
        a, b, dev = ((2, 1, nxt), (2, 3, prv), (1, 0, nxt), (3, 4, prv))[kind]
        part = pl.ds(p * half, half)
        return remote(
            xn.at[a, part], xn.at[b, part], halo_s.at[kind, p], halo_r.at[kind, p], dev
        )

    def gm_hop(kind, p):
        part = pl.ds(p * half, half)
        return remote(
            gm.at[kind, part], gm.at[kind + 1, part], gm_s.at[kind, p], gm_r.at[kind, p], prv
        )

    piece = core * nx + sx

    def shard_at(way, s):
        return lax.rem(pz - s + nz, nz) if way == 0 else lax.rem(pz + s, nz)

    def ring(way, s):
        ref = neg.at[shard_at(way, s), piece]
        return remote(
            ref, ref, ring_s.at[way, s], ring_r.at[way, s], at_z(1) if way == 0 else at_z(nz - 1)
        )

    def ring_arrived(way, s):
        ref = neg.at[shard_at(way, s + 1), piece]
        dev = at_z(1) if way == 0 else at_z(nz - 1)
        return remote(ref, ref, ring_s.at[way, s], ring_r.at[way, s], dev)

    def cross(way, s, k):
        to_a = (way == 0) == (k == 0)
        z = shard_at(way, s + 1)
        if way == 0 and k == 1:
            ref = neg.at[z, pl.ds(core * nx + 2 * lax.div(sx, 2), 2)]
        else:
            ref = neg.at[z, core * nx + (sx, sx, xb)[k]]
        return remote(ref, ref, xs_s.at[way, s, k], xs_r.at[way, s, k], dev_a if to_a else dev_b)

    def cross_arrived(way, s, k):
        z = shard_at(way, s + 1)
        if way == 0:
            ref = neg.at[z, core * nx + xa] if k == 0 else neg.at[z, pl.ds(core * nx + 2 * lax.div(xb, 2), 2)]
        else:
            ref = neg.at[z, core * nx + (xb, xa, nx - 1 - xa)[k]]
        to_a = (way == 0) == (k == 0)
        return remote(ref, ref, xs_s.at[way, s, k], xs_r.at[way, s, k], dev_a if to_a else dev_b)

    hops = ((1,), (1, 2))

    def sib_copy(way, s):
        ref = neg.at[shard_at(way, s + 1), pl.ds(core * nx, nx)]
        return remote(ref, ref, sib_s.at[way, s], sib_r.at[way, s], sib)

    def sib_arrived(way, s):
        ref = neg.at[shard_at(way, s + 1), pl.ds((1 - core) * nx, nx)]
        return remote(ref, ref, sib_s.at[way, s], sib_r.at[way, s], sib)

    def lp_copy(d):
        return remote(lpb.at[pz], lpb.at[pz], lp_s.at[d - 1], lp_r.at[d - 1], at_z(d))

    def lp_arrived(d):
        ref = lpb.at[lax.rem(pz - d + nz, nz)]
        return remote(ref, ref, lp_s.at[d - 1], lp_r.at[d - 1], at_z(d))

    loads[0].wait()
    raw = negs_raw[...].astype(F32)
    unit_neg = raw * lax.rsqrt(jnp.sum(raw * raw, axis=1, keepdims=True))
    neg[pz] = unit_neg.astype(BF16).reshape(neg.shape[1:])
    lpb[pz] = jnp.broadcast_to(lp_ref[...].astype(F32), lpb.shape[1:])
    loads[1].wait()
    own_x, inv_x = normalize(ev[...].astype(F32))
    normed_x[...] = own_x
    xn[2] = own_x.astype(BF16)

    pl.semaphore_wait(barrier, len(partners))

    for p in range(HALVES):
        halo(0, p).start()
        halo(1, p).start()
    ring(0, 0).start()
    if dns:
        ring(1, 0).start()
    for d in range(1, nz):
        lp_copy(d).start()

    def serve(way, s):
        ring_arrived(way, s).wait_recv()
        if s + 1 < (ups, dns)[way]:
            ring(way, s + 1).start()
        cross(way, s, 0).start()

    served = [0]

    def serve_next(count=1):
        for _ in range(count):
            s = served[0]
            for way in (0, 1):
                if s < (ups, dns)[way]:
                    serve(way, s)
            served[0] = s + 1

    def project_own(chunk, dst):
        def body(j, carry):
            cols = pl.ds(pl.multiple_of(j * cb, cb), cb)
            pre = dot(xn[2], win[chunk, :, cols])
            sg = jax.nn.sigmoid(pre)
            slopes[chunk, :, cols] = sg * (1.0 + pre * (1.0 - sg))
            dst[:, cols] = (pre * sg).astype(BF16)
            return carry

        lax.fori_loop(0, width // cb, body, 0)

    def project(slot, chunk, dst):
        def body(j, carry):
            cols = pl.ds(pl.multiple_of(j * cb, cb), cb)
            pre = dot(xn[slot], win[chunk, :, cols])
            dst[:, cols] = (pre * jax.nn.sigmoid(pre)).astype(BF16)
            return carry

        lax.fori_loop(0, width // cb, body, 0)

    loads[2].wait()
    project_own(2, kb.at[2])
    loads[3].wait()
    project_own(3, vb.at[2])

    for p in range(HALVES):
        halo(0, p).wait_recv()
        halo(2, p).start()
        halo(1, p).wait_recv()
        halo(3, p).start()
    serve_next()

    loads[4].wait()
    project_own(1, qb.at[0])
    loads[5].wait()
    project_own(0, upd)
    serve_next()

    users = lens_ref.shape[1]
    lens8 = jnp.broadcast_to(lens_ref[...].astype(F32), (8, users)).astype(BF16)
    ri = lax.broadcasted_iota(jnp.int32, (users, users), 0)
    ci = lax.broadcasted_iota(jnp.int32, (users, users), 1)
    before_cols = (ri < ci).astype(F32).astype(BF16)
    before_rows = (ci < ri).astype(F32).astype(BF16)
    starts_row = dot(lens8, before_cols)[0:1, :]
    starts_col = dot(before_rows, lens8, NT)[:, 0:1]
    first = (me * rows).astype(F32)
    own_pos = first + lax.broadcasted_iota(jnp.int32, (rows, 1), 0).astype(F32)
    own_first = jnp.max(jnp.where(starts_row <= own_pos, starts_row, 0.0), axis=1, keepdims=True)
    key_pos = first - 2.0 * rows + lax.broadcasted_iota(jnp.int32, (rows, 3 * rows), 1).astype(F32)
    mask_f[...] = jnp.where((key_pos >= own_first) & (key_pos <= own_pos), 1.0 / EV_DEV, 0.0)
    row_pos = first + lax.broadcasted_iota(jnp.int32, (1, 3 * rows), 1).astype(F32)
    row_first = jnp.max(jnp.where(starts_col <= row_pos, starts_col, 0.0), axis=0, keepdims=True)
    row_first = jnp.where(row_pos < events_all, row_first, float(2 * events_all))
    mask_t[...] = jnp.where((own_pos >= row_first) & (own_pos <= row_pos), 1.0 / EV_DEV, 0.0)
    serve_next()

    project(1, 2, kb.at[1])
    project(1, 3, vb.at[1])
    serve_next()
    project(3, 1, qb.at[1])
    serve_next()
    for p in range(HALVES):
        halo(2, p).wait_recv()
    project(0, 2, kb.at[0])
    project(0, 3, vb.at[0])
    serve_next(max(ups - 5, 0))

    for way in (0, 1):
        for s in range((ups, dns)[way]):
            cross_arrived(way, s, 0).wait_recv()
            for k in hops[way]:
                cross(way, s, k).start()

    def head_forward(h, carry):
        cols = pl.ds(pl.multiple_of(h * hw, hw), hw)
        keys = kb[:, :, cols].reshape(3 * rows, hw)
        values = vb[:, :, cols].reshape(3 * rows, hw)
        s = dot(qb[0, :, cols], keys, NT) * scale
        sg = jax.nn.sigmoid(s)
        seen = mask_f[...]
        sc_slope[h] = seen * (sg * (1.0 + s * (1.0 - sg)))
        w = (s * sg * seen).astype(BF16)
        mixed[:, cols] = dot(w, values)
        return carry

    lax.fori_loop(0, heads, head_forward, 0)

    for way in (0, 1):
        for s in range((ups, dns)[way]):
            for k in hops[way]:
                cross_arrived(way, s, k).wait_recv()
            sib_copy(way, s).start()

    normed_o, inv_o = normalize(mixed[...])
    mixed[...] = normed_o
    gated = normed_o * upd[...].astype(F32)
    gated_low = gated.astype(BF16)
    x_rows = ev[...].astype(F32)
    loads[6].wait()
    layer_out = dot(gated_low, wout[...]) + x_rows
    inv_norm = lax.rsqrt(jnp.sum(layer_out * layer_out, axis=1, keepdims=True))
    unit_out = layer_out * inv_norm
    unit[...] = unit_out
    unit_low = unit_out.astype(BF16)

    per_y = width // ny
    for j in range(ny):
        turned = gated[:, j * per_y : (j + 1) * per_y].T.astype(BF16)
        for c in range(2):
            for k in range(nx):
                r0 = (c * nx + k) * out_rows
                gt[c, k, j] = turned[r0 : r0 + out_rows]
    to_sib_g = remote(gt.at[1 - core], gt_sib, pair_s.at[0], pair_r.at[0], sib)
    to_sib_g.start()

    loads[7].wait()
    pos_rows = pos[...].astype(F32)
    pos_unit = pos_rows * lax.rsqrt(jnp.sum(pos_rows * pos_rows, axis=1, keepdims=True))
    pos_exp = jnp.exp(jnp.sum(unit_out * pos_unit, axis=1, keepdims=True) / sharpness_divisor)

    for d in range(1, nz):
        lp_arrived(d).wait_recv()
    for way in (0, 1):
        for s in range((ups, dns)[way]):
            sib_arrived(way, s).wait_recv()

    def logits(z, exp_total):
        negs = neg[z].reshape(rows, width)
        lg = dot(unit_low, negs, NT) * (1.0 / sharpness_divisor) - lpb[z, 0:1, :]
        e = jnp.exp(lg)
        ebuf[:, pl.ds(pl.multiple_of(z * rows, rows), rows)] = e.astype(BF16)
        return exp_total + jnp.sum(e, axis=1, keepdims=True)

    exp_total = lax.fori_loop(0, nz, logits, jnp.zeros((rows, 1), F32))
    denominator = pos_exp + exp_total
    mixed_negs = dot(ebuf[...], neg[...].reshape(nz * rows, width))
    unit_out = unit[...]
    grad_unit = (
        loss_multiplier
        / sharpness_divisor
        * (mixed_negs / denominator + (pos_exp / denominator - 1.0) * pos_unit)
    )
    grad_out = (
        grad_unit - unit_out * jnp.sum(unit_out * grad_unit, axis=1, keepdims=True)
    ) * inv_norm
    gout[...] = grad_out
    gl2[0] = grad_out.astype(BF16)
    to_sib_l = remote(gl2.at[0], gl2.at[1], pair_s.at[1], pair_r.at[1], sib)
    to_sib_l.start()

    def gate_back(j, carry):
        cols = pl.ds(pl.multiple_of(j * cb, cb), cb)
        gact[:, cols] = dot(gl2[0], wout[cols, :], NT)
        return carry

    lax.fori_loop(0, width // cb, gate_back, 0)
    grad_gated = gact[...]
    normed_o = mixed[...]
    gpre[:, 0:width] = (grad_gated * normed_o * slopes[0]).astype(BF16)
    gm[0] = norm_back(grad_gated * upd[...].astype(F32), normed_o, inv_o).astype(BF16)
    for p in range(HALVES):
        gm_hop(0, p).start()

    to_sib_g.wait_recv()
    to_sib_l.wait_recv()

    def weight_part(k):
        mine = gt[core, k].reshape(ny * out_rows, rows)
        theirs = gt_sib[k].reshape(ny * out_rows, rows)
        left = jnp.concatenate([mine, theirs], axis=1)
        return dot(left, gl2[...].reshape(2 * rows, width))

    wide = width // 2

    def dwx(side, i):
        return remote(
            send_a.at[side, i], recv_x.at[side, i], dwx_s.at[side, i], dwx_r.at[side, i], (dev_a, dev_b)[side]
        )

    def dwx2(side):
        return remote(
            send_a2.at[side], recv_x2.at[side], dwx_s.at[side, 2], dwx_r.at[side, 2], (dev_b, dev_a)[side]
        )

    part = weight_part(lax.rem(sx + 2, nx))
    for side in (0, 1):
        send_a[side, 0] = part[:, side * wide : (side + 1) * wide].astype(BF16).reshape(send_a.shape[2:])
        dwx(side, 0).start()
    for side, at in ((0, xa), (1, xb)):
        part = weight_part(at)
        send_a[side, 1] = part[:, side * wide : (side + 1) * wide].astype(BF16).reshape(send_a.shape[2:])
        dwx(side, 1).start()
        part_x[1 - side] = part[:, (1 - side) * wide : (2 - side) * wide].reshape(part_x.shape[1:])
    own_b[...] = weight_part(sx).reshape(own_b.shape)

    def head_query(h, carry):
        cols = pl.ds(pl.multiple_of(h * hw, hw), hw)
        values = vb[:, :, cols].reshape(3 * rows, hw)
        keys = kb[:, :, cols].reshape(3 * rows, hw)
        gs = (dot(gm[0, :, cols], values, NT) * sc_slope[h]).astype(BF16)
        gq = dot(gs, keys) * scale
        at = pl.ds(pl.multiple_of(width + h * hw, hw), hw)
        gpre[:, at] = (gq * slopes[1, :, cols]).astype(BF16)
        return carry

    lax.fori_loop(0, heads, head_query, 0)

    for p in range(HALVES):
        gm_hop(0, p).wait_recv()
        gm_hop(1, p).start()

    def dwy(d):
        return remote(
            send_b.at[lax.rem(yy + d, ny)], recv_y.at[d - 1], dwy_s.at[d - 1], dwy_r.at[d - 1], at_y(d)
        )

    def head_keys(lo, count):
        def body(h, carry):
            cols = pl.ds(pl.multiple_of(h * hw, hw), hw)
            queries = qb[lo : lo + count, :, cols].reshape(count * rows, hw)
            grads = gm[lo : lo + count, :, cols].reshape(count * rows, hw)
            s = dot(kb[2, :, cols], queries, NT) * scale
            sg = jax.nn.sigmoid(s)
            seen = mask_t[:, lo * rows : (lo + count) * rows]
            w = (s * sg * seen).astype(BF16)
            gv = dot(w, grads)
            gs = (dot(vb[2, :, cols], grads, NT) * seen * (sg * (1.0 + s * (1.0 - sg)))).astype(BF16)
            gk = dot(gs, queries)
            if lo == 0:
                gvals[:, cols] = gv
                gkeys[:, cols] = gk
                return carry
            gv = gv + gvals[:, cols]
            gk = (gk + gkeys[:, cols]) * scale
            at = pl.ds(pl.multiple_of(2 * width + h * hw, hw), hw)
            gpre[:, at] = (gk * slopes[2, :, cols]).astype(BF16)
            at = pl.ds(pl.multiple_of(3 * width + h * hw, hw), hw)
            gpre[:, at] = (gv * slopes[3, :, cols]).astype(BF16)
            return carry

        lax.fori_loop(0, heads, body, 0)

    head_keys(0, 2)

    for side in (0, 1):
        dwx(side, 0).wait_recv()
        send_a2[side] = (part_x[side] + recv_x[side, 0].astype(F32)).astype(BF16)
        dwx2(side).start()

    for p in range(HALVES):
        halo(3, p).wait_recv()
    project(4, 1, qb.at[2])
    for p in range(HALVES):
        gm_hop(1, p).wait_recv()
    head_keys(2, 1)

    for side in (0, 1):
        dwx(side, 1).wait_recv()
        dwx2(side).wait_recv()
        half_cols = pl.ds(side * wide, wide)
        summed = own_b[:, :, half_cols] + recv_x[side, 1].astype(F32) + recv_x2[side].astype(F32)
        own_b[:, :, half_cols] = summed
        send_b[:, :, half_cols] = summed.astype(BF16)
    for d in range(1, ny):
        dwy(d).start()

    def x_back(j, carry):
        cols = pl.ds(pl.multiple_of(j * cb, cb), cb)
        part = dot(gpre[:, 0:width], win[0, cols, :], NT)
        for c in range(1, 4):
            part = part + dot(gpre[:, c * width : (c + 1) * width], win[c, cols, :], NT)
        gact[:, cols] = part
        return carry

    lax.fori_loop(0, width // cb, x_back, 0)
    dout[...] = norm_back(gact[...], normed_x[...], inv_x) + gout[...]
    out_copy = pltpu.make_async_copy(dout, dev_hbm, load_sem.at[8])
    out_copy.start()

    def dwz(d):
        return remote(
            send_c.at[lax.rem(pz + d, nz)], recv_z.at[d - 1], dwz_s.at[d - 1], dwz_r.at[d - 1], at_z(d)
        )

    def dwz_arrived(d):
        return remote(send_c.at[0], recv_z.at[d - 1], dwz_s.at[d - 1], dwz_r.at[d - 1], at_z(d))

    def fin_copy(d):
        return remote(fin.at[pz], fin.at[pz], fin_s.at[d - 1], fin_r.at[d - 1], at_z(d))

    def fin_arrived(d):
        ref = fin.at[lax.rem(pz - d + nz, nz)]
        return remote(ref, ref, fin_s.at[d - 1], fin_r.at[d - 1], at_z(d))

    for d in range(1, ny):
        dwy(d).wait_recv()
    summed = own_b[yy]
    for d in range(1, ny):
        summed = summed + recv_y[d - 1].astype(F32)
    for t in range(reds):
        own_c[t] = summed[:, t * tw : (t + 1) * tw]
        send_c[t] = summed[:, t * tw : (t + 1) * tw].astype(BF16)
    for d in range(1, nz):

        @pl.when(lax.rem(pz + d, nz) < reds)
        def _(d=d):
            dwz(d).start()

    @pl.when(pz < reds)
    def _():
        for d in range(1, nz):
            dwz_arrived(d).wait_recv()
        done = own_c[pz]
        for d in range(1, nz):
            done = done + recv_z[d - 1].astype(F32)
        fin[pz] = done
        for d in range(1, nz):
            fin_copy(d).start()

    for d in range(1, nz):

        @pl.when(lax.rem(pz - d + nz, nz) < reds)
        def _(d=d):
            fin_arrived(d).wait_recv()

    for t in range(reds):
        dw_ref[:, t * tw : (t + 1) * tw] = fin[t]
    out_copy.wait()

    for p in range(HALVES):
        for kind in range(4):
            halo(kind, p).wait_send()
        for kind in range(2):
            gm_hop(kind, p).wait_send()
    for way in (0, 1):
        for s in range((ups, dns)[way]):
            ring(way, s).wait_send()
            for k in (0, *hops[way]):
                cross(way, s, k).wait_send()
            sib_copy(way, s).wait_send()
    for d in range(1, nz):
        lp_copy(d).wait_send()
    to_sib_g.wait_send()
    to_sib_l.wait_send()
    for side in (0, 1):
        dwx(side, 0).wait_send()
        dwx(side, 1).wait_send()
        dwx2(side).wait_send()
    for d in range(1, ny):
        dwy(d).wait_send()
    for d in range(1, nz):

        @pl.when(lax.rem(pz + d, nz) < reds)
        def _(d=d):
            dwz(d).wait_send()

    @pl.when(pz < reds)
    def _():
        for d in range(1, nz):
            fin_copy(d).wait_send()


def shards(mesh_sizes, events, input_weight, output_weight, positives, negatives, log_probs, lengths):
    ndp, nx, nz = mesh_sizes
    ny = ndp // 2
    rows, width = events.shape
    heads = HEADS
    users = lengths.shape[0]
    ups = nz // 2
    reds = 8 if nz >= 8 else 2
    tw = width // reds
    out_rows = width // (ndp * nx)
    piece_rows = rows // (2 * nx)
    events_all = rows * ndp * nx * nz
    lens = lengths.reshape(1, users)
    lps = log_probs.reshape(1, rows)
    v = pltpu.VMEM
    dma = pltpu.SemaphoreType.DMA
    scratch = [
        v((rows, width), BF16),
        v((4, width, width), BF16),
        v((width, width), BF16),
        v((rows, width), BF16),
        v((rows, width), BF16),
        v((5, rows, width), BF16),
        v((rows, width), F32),
        v((4, rows, width), F32),
        v((rows, width), BF16),
        v((3, rows, width), BF16),
        v((3, rows, width), BF16),
        v((3, rows, width), BF16),
        v((rows, 3 * rows), F32),
        v((rows, 3 * rows), F32),
        v((heads, rows, 3 * rows), F32),
        v((rows, width), F32),
        v((nz, 2 * nx, piece_rows, width), BF16),
        v((nz, 8, rows), F32),
        v((rows, nz * rows), BF16),
        v((rows, width), F32),
        v((rows, width), F32),
        v((2, rows, width), BF16),
        v((2, nx, ny, out_rows, rows), BF16),
        v((nx, ny, out_rows, rows), BF16),
        v((3, rows, width), BF16),
        v((rows, width), F32),
        v((rows, 4 * width), BF16),
        v((rows, width), F32),
        v((rows, width), F32),
        v((rows, width), F32),
        v((2, 2, ny, out_rows, width // 2), BF16),
        v((2, 2, ny, out_rows, width // 2), BF16),
        v((2, ny, out_rows, width // 2), BF16),
        v((2, ny, out_rows, width // 2), BF16),
        v((2, ny, out_rows, width // 2), F32),
        v((ny, out_rows, width), F32),
        v((ny, out_rows, width), BF16),
        v((ny - 1, out_rows, width), BF16),
        v((reds, out_rows, tw), F32),
        v((reds, out_rows, tw), BF16),
        v((nz - 1, out_rows, tw), BF16),
        v((reds, out_rows, tw), F32),
        dma((9,)),
        dma((4, HALVES)),
        dma((4, HALVES)),
        dma((2, HALVES)),
        dma((2, HALVES)),
        dma((2, ups)),
        dma((2, ups)),
        dma((2, ups, 3)),
        dma((2, ups, 3)),
        dma((2, ups)),
        dma((2, ups)),
        dma((nz - 1,)),
        dma((nz - 1,)),
        dma((2,)),
        dma((2,)),
        dma((2, 3)),
        dma((2, 3)),
        dma((ny - 1,)),
        dma((ny - 1,)),
        dma((nz - 1,)),
        dma((nz - 1,)),
        dma((nz - 1,)),
        dma((nz - 1,)),
    ]
    hbm = pl.BlockSpec(memory_space=pl.ANY)
    vmem = pl.BlockSpec(memory_space=pltpu.VMEM)
    return pl.pallas_call(
        functools.partial(kernel, (ny, nx, nz, width, heads, events_all)),
        out_shape=(
            jax.ShapeDtypeStruct((rows, width), F32),
            jax.ShapeDtypeStruct((out_rows, width), F32),
        ),
        in_specs=[vmem, vmem, hbm, hbm, hbm, hbm, hbm],
        out_specs=(hbm, vmem),
        scratch_shapes=scratch,
        compiler_params=pltpu.CompilerParams(
            collective_id=0, has_side_effects=True, vmem_limit_bytes=56 * 1024 * 1024
        ),
    )(lens, lps, events, input_weight, output_weight, positives, negatives)


def solution(mesh):
    sizes = tuple(mesh.shape[a] for a in AXES)
    placed = (
        P(AXES, None),
        P(),
        P(),
        P(AXES, None),
        P("pool", None),
        P("pool"),
        P(),
    )
    return jax.shard_map(
        functools.partial(shards, sizes),
        mesh=mesh,
        in_specs=placed,
        out_specs=(P(AXES, None), P(("dp", "seq"), None)),
        check_vma=False,
    )
```

```python
import functools
import math

import jax
import jax.numpy as jnp
from jax import lax
from jax.experimental import pallas as pl
from jax.experimental.pallas import tpu as pltpu
from jax.sharding import PartitionSpec as P

HEADS = 8
EV_DEV = 128

epsilon = 1e-05
sharpness_divisor = 0.05
loss_multiplier = 8.0

MESH = pl.DeviceIdType.MESH
AXES = ("dp", "seq", "pool")
NT = (((1,), (1,)), ((), ()))
NN = (((1,), (0,)), ((), ()))
HALVES = 2
F32 = jnp.float32
BF16 = jnp.bfloat16


def dot(a, b, dims=NN):
    return lax.dot_general(a, b, dims, preferred_element_type=F32)


def slope(v):
    sg = jax.nn.sigmoid(v)
    return sg * (1.0 + v * (1.0 - sg))


def mean_last(v):
    return jnp.mean(v, axis=1, keepdims=True)


def normalize(row_data):
    centred = row_data - mean_last(row_data)
    inv_std = lax.rsqrt(mean_last(centred * centred) + epsilon)
    return centred * inv_std, inv_std


def norm_back(grad_in, normed, inv_std):
    return (grad_in - mean_last(grad_in) - normed * mean_last(grad_in * normed)) * inv_std


def kernel(
    sizes,
    lens_ref,
    lp_ref,
    ev_hbm,
    win_hbm,
    wout_hbm,
    pos_hbm,
    neg_hbm,
    dev_hbm,
    dw_ref,
    ev,
    win,
    wout,
    pos,
    negs_raw,
    xn,
    normed_x,
    slopes,
    upd,
    qb,
    kb,
    vb,
    mask_f,
    mask_t,
    sc_slope,
    mixed,
    neg,
    lpb,
    ebuf,
    unit,
    gout,
    gl2,
    gt,
    gt_sib,
    gm,
    gact,
    gpre,
    dout,
    gkeys,
    gvals,
    send_a,
    recv_x,
    send_a2,
    recv_x2,
    part_x,
    own_b,
    send_b,
    recv_y,
    line_a,
    line_b,
    load_sem,
    halo_s,
    halo_r,
    gm_s,
    gm_r,
    ring_s,
    ring_r,
    xs_s,
    xs_r,
    sib_s,
    sib_r,
    lp_s,
    lp_r,
    pair_s,
    pair_r,
    dwx_s,
    dwx_r,
    dwy_s,
    dwy_r,
    dwz_s,
    dwz_r,
    fin_s,
    fin_r,
):
    ny, nx, nz, width, heads, events_all = sizes
    hw = width // heads
    rows = EV_DEV
    cb = 256
    inner, outer = line_a.shape[0], line_b.shape[0]
    out_rows = line_a.shape[1]
    scale = 1.0 / math.sqrt(hw)

    dp = lax.axis_index("dp")
    sx = lax.axis_index("seq")
    pz = lax.axis_index("pool")
    core = lax.rem(dp, 2)
    yy = lax.div(dp, 2)
    other = dp + 1 - 2 * core
    total = 2 * ny * nx * nz
    me = (dp * nx + sx) * nz + pz

    def place(i):
        return (lax.div(i, nx * nz), lax.rem(lax.div(i, nz), nx), lax.rem(i, nz))

    nxt = place(lax.rem(me + 1, total))
    prv = place(lax.rem(me + total - 1, total))
    sib = (other, sx, pz)

    xa = sx + 1 - 2 * lax.rem(sx, 2)
    xb = nx - 1 - sx
    dev_a = (dp, xa, pz)
    dev_b = (dp, xb, pz)

    def at_y(d):
        return (lax.rem(yy + d, ny) * 2 + core, sx, pz)

    def at_z(d):
        return (dp, sx, lax.rem(pz + d, nz))

    def load(i, src, dst):
        return pltpu.make_async_copy(src, dst, load_sem.at[i])

    def remote(src, dst, s, r, dev):
        return pltpu.make_async_remote_copy(
            src_ref=src, dst_ref=dst, send_sem=s, recv_sem=r, device_id=dev, device_id_type=MESH
        )

    loads = [
        load(0, neg_hbm, negs_raw),
        load(1, ev_hbm, ev),
        load(2, win_hbm.at[:, pl.ds(2 * width, width)], win.at[2]),
        load(3, win_hbm.at[:, pl.ds(3 * width, width)], win.at[3]),
        load(4, win_hbm.at[:, pl.ds(width, width)], win.at[1]),
        load(5, win_hbm.at[:, pl.ds(0, width)], win.at[0]),
        load(6, wout_hbm, wout),
        load(7, pos_hbm, pos),
    ]
    for item in loads:
        item.start()

    barrier = pltpu.get_barrier_semaphore()
    partners = [nxt, prv, sib]
    partners += [dev_a, dev_b]
    partners += [at_y(d) for d in range(1, ny)]
    partners += [at_z(d) for d in range(1, nz)]
    for partner in partners:
        pl.semaphore_signal(barrier, inc=1, device_id=partner, device_id_type=MESH)

    half = rows // HALVES

    def halo(kind, p):
        a, b, dev = ((2, 1, nxt), (2, 3, prv), (1, 0, nxt), (3, 4, prv))[kind]
        part = pl.ds(p * half, half)
        return remote(
            xn.at[a, part], xn.at[b, part], halo_s.at[kind, p], halo_r.at[kind, p], dev
        )

    def gm_hop(kind, p):
        part = pl.ds(p * half, half)
        return remote(
            gm.at[kind, part], gm.at[kind + 1, part], gm_s.at[kind, p], gm_r.at[kind, p], prv
        )

    colour = lax.rem(sx + 2 * yy, nx)
    piece = core * nx + colour
    hops = sorted(range(1, nz), key=lambda d: (min(d, nz - d), d))
    dev_up = (dp, lax.rem(sx + 1, nx), pz)
    dev_down = (dp, lax.rem(sx + nx - 1, nx), pz)

    near = nz // 2
    batches = (pl.ds(1, near), pl.ds(1 + near, nz - 1 - near))

    def ring(i):
        b = 0 if i < near else 1
        return remote(
            neg.at[0, piece], neg.at[i + 1, piece], ring_s.at[b], ring_r.at[b], at_z(hops[i])
        )

    def ring_all(b):
        ref = neg.at[batches[b], piece]
        return remote(ref, ref, ring_s.at[b], ring_r.at[b], at_z(1))

    def cross(b, k, slot=None):
        ref = neg.at[batches[b], piece if slot is None else slot]
        dev = (dev_up, dev_down, at_y((1, ny - 1)[b]))[k]
        return remote(ref, ref, xs_s.at[b, k], xs_r.at[b, k], dev)

    def cross_arrived(b, k):
        return cross(b, k, core * nx + lax.rem(colour + (3, 1, 2)[k], nx))

    def sib_copy(b):
        ref = neg.at[batches[b], pl.ds(core * nx, nx)]
        return remote(ref, ref, sib_s.at[b], sib_r.at[b], sib)

    def sib_arrived(b):
        ref = neg.at[batches[b], pl.ds((1 - core) * nx, nx)]
        return remote(ref, ref, sib_s.at[b], sib_r.at[b], sib)

    def lp_copy(i):
        return remote(lpb.at[0], lpb.at[i + 1], lp_s.at[0], lp_r.at[0], at_z(hops[i]))

    def lp_all():
        ref = lpb.at[pl.ds(1, nz - 1)]
        return remote(ref, ref, lp_s.at[0], lp_r.at[0], at_z(1))

    loads[0].wait()
    raw = negs_raw[...].astype(F32)
    unit_neg = raw * lax.rsqrt(jnp.sum(raw * raw, axis=1, keepdims=True))
    neg[0] = unit_neg.astype(BF16).reshape(neg.shape[1:])
    lpb[0] = jnp.broadcast_to(lp_ref[...].astype(F32), lpb.shape[1:])
    loads[1].wait()
    own_x, inv_x = normalize(ev[...].astype(F32))
    normed_x[...] = own_x
    xn[2] = own_x.astype(BF16)

    pl.semaphore_wait(barrier, len(partners))

    for p in range(HALVES):
        halo(0, p).start()
        halo(1, p).start()

    def serve(b):
        ring_all(b).wait_recv()
        for k in range(3):
            cross(b, k).start()

    def pass_on(b):
        for k in range(3):
            cross_arrived(b, k).wait_recv()
        sib_copy(b).start()

    def project_own(chunk, dst):
        def body(j, carry):
            cols = pl.ds(pl.multiple_of(j * cb, cb), cb)
            pre = dot(xn[2], win[chunk, :, cols])
            sg = jax.nn.sigmoid(pre)
            slopes[chunk, :, cols] = sg * (1.0 + pre * (1.0 - sg))
            dst[:, cols] = (pre * sg).astype(BF16)
            return carry

        lax.fori_loop(0, width // cb, body, 0)

    def project(slot, chunk, dst):
        def body(j, carry):
            cols = pl.ds(pl.multiple_of(j * cb, cb), cb)
            pre = dot(xn[slot], win[chunk, :, cols])
            dst[:, cols] = (pre * jax.nn.sigmoid(pre)).astype(BF16)
            return carry

        lax.fori_loop(0, width // cb, body, 0)

    loads[2].wait()
    project_own(2, kb.at[2])
    loads[3].wait()
    project_own(3, vb.at[2])

    for p in range(HALVES):
        halo(0, p).wait_recv()
        halo(2, p).start()
        halo(1, p).wait_recv()
        halo(3, p).start()
    for i in range(nz - 1):
        ring(i).start()
    for i in range(nz - 1):
        lp_copy(i).start()

    loads[4].wait()
    project_own(1, qb.at[0])
    loads[5].wait()
    project_own(0, upd)

    lens_rows, lens_cols = lens_ref.shape
    users = lens_rows * lens_cols
    lens_line = jnp.concatenate([lens_ref[k : k + 1, :] for k in range(lens_rows)], axis=1)
    lens8 = jnp.broadcast_to(lens_line.astype(F32), (8, users)).astype(BF16)
    ri = lax.broadcasted_iota(jnp.int32, (users, users), 0)
    ci = lax.broadcasted_iota(jnp.int32, (users, users), 1)
    before_cols = (ri < ci).astype(F32).astype(BF16)
    before_rows = (ci < ri).astype(F32).astype(BF16)
    starts_row = dot(lens8, before_cols)[0:1, :]
    starts_col = dot(before_rows, lens8, NT)[:, 0:1]
    first = (me * rows).astype(F32)
    own_pos = first + lax.broadcasted_iota(jnp.int32, (rows, 1), 0).astype(F32)
    own_first = jnp.max(jnp.where(starts_row <= own_pos, starts_row, 0.0), axis=1, keepdims=True)
    key_pos = first - 2.0 * rows + lax.broadcasted_iota(jnp.int32, (rows, 3 * rows), 1).astype(F32)
    mask_f[...] = jnp.where((key_pos >= own_first) & (key_pos <= own_pos), 1.0 / EV_DEV, 0.0)
    row_pos = first + lax.broadcasted_iota(jnp.int32, (1, 3 * rows), 1).astype(F32)
    row_first = jnp.max(jnp.where(starts_col <= row_pos, starts_col, 0.0), axis=0, keepdims=True)
    row_first = jnp.where(row_pos < events_all, row_first, float(2 * events_all))
    mask_t[...] = jnp.where((own_pos >= row_first) & (own_pos <= row_pos), 1.0 / EV_DEV, 0.0)

    project(1, 2, kb.at[1])
    project(1, 3, vb.at[1])
    project(3, 1, qb.at[1])
    for p in range(HALVES):
        halo(2, p).wait_recv()
    serve(0)
    project(0, 2, kb.at[0])
    project(0, 3, vb.at[0])

    def head_forward(h, carry):
        cols = pl.ds(pl.multiple_of(h * hw, hw), hw)
        keys = kb[:, :, cols].reshape(3 * rows, hw)
        values = vb[:, :, cols].reshape(3 * rows, hw)
        s = dot(qb[0, :, cols], keys, NT) * scale
        sg = jax.nn.sigmoid(s)
        seen = mask_f[...]
        sc_slope[h] = seen * (sg * (1.0 + s * (1.0 - sg)))
        w = (s * sg * seen).astype(BF16)
        mixed[:, cols] = dot(w, values)
        return carry

    lax.fori_loop(0, heads, head_forward, 0)

    serve(1)

    normed_o, inv_o = normalize(mixed[...])
    mixed[...] = normed_o
    gated = normed_o * upd[...].astype(F32)
    gated_low = gated.astype(BF16)
    x_rows = ev[...].astype(F32)
    loads[6].wait()
    layer_out = dot(gated_low, wout[...]) + x_rows
    inv_norm = lax.rsqrt(jnp.sum(layer_out * layer_out, axis=1, keepdims=True))
    unit_out = layer_out * inv_norm
    unit[...] = unit_out
    unit_low = unit_out.astype(BF16)

    pass_on(0)

    per_y = width // ny
    for j in range(ny):
        turned = gated[:, j * per_y : (j + 1) * per_y].T.astype(BF16)
        for c in range(2):
            for k in range(nx):
                r0 = (c * nx + k) * out_rows
                gt[c, k, j] = turned[r0 : r0 + out_rows]
    to_sib_g = remote(gt.at[1 - core], gt_sib, pair_s.at[0], pair_r.at[0], sib)
    to_sib_g.start()

    loads[7].wait()
    pos_rows = pos[...].astype(F32)
    pos_unit = pos_rows * lax.rsqrt(jnp.sum(pos_rows * pos_rows, axis=1, keepdims=True))
    pos_exp = jnp.exp(jnp.sum(unit_out * pos_unit, axis=1, keepdims=True) / sharpness_divisor)

    pass_on(1)
    lp_all().wait_recv()
    def logits(z, exp_total):
        negs = neg[z].reshape(rows, width)
        lg = dot(unit_low, negs, NT) * (1.0 / sharpness_divisor) - lpb[z, 0:1, :]
        e = jnp.exp(lg)
        ebuf[:, pl.ds(pl.multiple_of(z * rows, rows), rows)] = e.astype(BF16)
        return exp_total + jnp.sum(e, axis=1, keepdims=True)

    exp_total = logits(0, jnp.zeros((rows, 1), F32))
    for b, (lo, hi) in enumerate(((1, 1 + near), (1 + near, nz))):
        sib_arrived(b).wait_recv()
        exp_total = lax.fori_loop(lo, hi, logits, exp_total)
    denominator = pos_exp + exp_total
    mixed_negs = dot(ebuf[...], neg[...].reshape(nz * rows, width))
    unit_out = unit[...]
    grad_unit = (
        loss_multiplier
        / sharpness_divisor
        * (mixed_negs / denominator + (pos_exp / denominator - 1.0) * pos_unit)
    )
    grad_out = (
        grad_unit - unit_out * jnp.sum(unit_out * grad_unit, axis=1, keepdims=True)
    ) * inv_norm
    gout[...] = grad_out
    gl2[0] = grad_out.astype(BF16)
    to_sib_l = remote(gl2.at[0], gl2.at[1], pair_s.at[1], pair_r.at[1], sib)
    to_sib_l.start()

    def gate_back(j, carry):
        cols = pl.ds(pl.multiple_of(j * cb, cb), cb)
        gact[:, cols] = dot(gl2[0], wout[cols, :], NT)
        return carry

    lax.fori_loop(0, width // cb, gate_back, 0)
    grad_gated = gact[...]
    normed_o = mixed[...]
    gpre[:, 0:width] = (grad_gated * normed_o * slopes[0]).astype(BF16)
    gm[0] = norm_back(grad_gated * upd[...].astype(F32), normed_o, inv_o).astype(BF16)
    for p in range(HALVES):
        gm_hop(0, p).start()

    to_sib_g.wait_recv()
    to_sib_l.wait_recv()

    def weight_part(k):
        mine = gt[core, k].reshape(ny * out_rows, rows)
        theirs = gt_sib[k].reshape(ny * out_rows, rows)
        left = jnp.concatenate([mine, theirs], axis=1)
        return dot(left, gl2[...].reshape(2 * rows, width))

    wide = width // 2

    def dwx(side, i):
        return remote(
            send_a.at[side, i], recv_x.at[side, i], dwx_s.at[side, i], dwx_r.at[side, i], (dev_a, dev_b)[side]
        )

    def dwx2(side):
        return remote(
            send_a2.at[side], recv_x2.at[side], dwx_s.at[side, 2], dwx_r.at[side, 2], (dev_b, dev_a)[side]
        )

    part = weight_part(lax.rem(sx + 2, nx))
    for side in (0, 1):
        send_a[side, 0] = part[:, side * wide : (side + 1) * wide].astype(BF16).reshape(send_a.shape[2:])
        dwx(side, 0).start()
    for side, at in ((0, xa), (1, xb)):
        part = weight_part(at)
        send_a[side, 1] = part[:, side * wide : (side + 1) * wide].astype(BF16).reshape(send_a.shape[2:])
        dwx(side, 1).start()
        part_x[1 - side] = part[:, (1 - side) * wide : (2 - side) * wide].reshape(part_x.shape[1:])
    own_b[...] = weight_part(sx).reshape(own_b.shape)

    def head_query(h, carry):
        cols = pl.ds(pl.multiple_of(h * hw, hw), hw)
        values = vb[:, :, cols].reshape(3 * rows, hw)
        keys = kb[:, :, cols].reshape(3 * rows, hw)
        gs = (dot(gm[0, :, cols], values, NT) * sc_slope[h]).astype(BF16)
        gq = dot(gs, keys) * scale
        at = pl.ds(pl.multiple_of(width + h * hw, hw), hw)
        gpre[:, at] = (gq * slopes[1, :, cols]).astype(BF16)
        return carry

    lax.fori_loop(0, heads, head_query, 0)

    for p in range(HALVES):
        gm_hop(0, p).wait_recv()
        gm_hop(1, p).start()

    def dwy(d):
        return remote(
            send_b.at[lax.rem(yy + d, ny)], recv_y.at[d - 1], dwy_s.at[0], dwy_r.at[0], at_y(d)
        )

    def dwy_all():
        return remote(recv_y, recv_y, dwy_s.at[0], dwy_r.at[0], at_y(1))

    def head_keys(lo, count):
        def body(h, carry):
            cols = pl.ds(pl.multiple_of(h * hw, hw), hw)
            queries = qb[lo : lo + count, :, cols].reshape(count * rows, hw)
            grads = gm[lo : lo + count, :, cols].reshape(count * rows, hw)
            s = dot(kb[2, :, cols], queries, NT) * scale
            sg = jax.nn.sigmoid(s)
            seen = mask_t[:, lo * rows : (lo + count) * rows]
            w = (s * sg * seen).astype(BF16)
            gv = dot(w, grads)
            gs = (dot(vb[2, :, cols], grads, NT) * seen * (sg * (1.0 + s * (1.0 - sg)))).astype(BF16)
            gk = dot(gs, queries)
            if lo == 0:
                gvals[:, cols] = gv
                gkeys[:, cols] = gk
                return carry
            gv = gv + gvals[:, cols]
            gk = (gk + gkeys[:, cols]) * scale
            at = pl.ds(pl.multiple_of(2 * width + h * hw, hw), hw)
            gpre[:, at] = (gk * slopes[2, :, cols]).astype(BF16)
            at = pl.ds(pl.multiple_of(3 * width + h * hw, hw), hw)
            gpre[:, at] = (gv * slopes[3, :, cols]).astype(BF16)
            return carry

        lax.fori_loop(0, heads, body, 0)

    head_keys(0, 2)

    for side in (0, 1):
        dwx(side, 0).wait_recv()
        send_a2[side] = (part_x[side] + recv_x[side, 0].astype(F32)).astype(BF16)
        dwx2(side).start()

    for p in range(HALVES):
        halo(3, p).wait_recv()
    project(4, 1, qb.at[2])
    for p in range(HALVES):
        gm_hop(1, p).wait_recv()
    head_keys(2, 1)

    for side in (0, 1):
        dwx(side, 1).wait_recv()
        dwx2(side).wait_recv()
        half_cols = pl.ds(side * wide, wide)
        summed = own_b[:, :, half_cols] + recv_x[side, 1].astype(F32) + recv_x2[side].astype(F32)
        own_b[:, :, half_cols] = summed
        send_b[:, :, half_cols] = summed.astype(BF16)
    for d in range(1, ny):
        dwy(d).start()

    def x_back(j, carry):
        cols = pl.ds(pl.multiple_of(j * cb, cb), cb)
        part = dot(gpre[:, 0:width], win[0, cols, :], NT)
        for c in range(1, 4):
            part = part + dot(gpre[:, c * width : (c + 1) * width], win[c, cols, :], NT)
        gact[:, cols] = part
        return carry

    lax.fori_loop(0, width // cb, x_back, 0)
    dout[...] = norm_back(gact[...], normed_x[...], inv_x) + gout[...]
    out_copy = pltpu.make_async_copy(dout, dev_hbm, load_sem.at[8])
    out_copy.start()

    row_a, row_b = lax.rem(pz, inner), lax.div(pz, inner)

    def line(which, d, source=False):
        count = (inner, outer)[which]
        spot = (row_a, row_b)[which]
        there = lax.rem(spot + (count - d if source else d), count)
        to = lax.rem(spot + d, count)
        buf = (line_a, line_b)[which]
        ref = buf.at[there if source else spot]
        dev = (dp, sx, row_b * inner + to) if which == 0 else (dp, sx, to * inner + row_a)
        return remote(ref, ref, (dwz_s, fin_s)[which].at[d - 1], (dwz_r, fin_r)[which].at[d - 1], dev)

    dwy_all().wait_recv()
    summed = own_b[yy]
    for d in range(1, ny):
        summed = summed + recv_y[d - 1].astype(F32)
    for which in (0, 1):
        buf, count = ((line_a, inner), (line_b, outer))[which]
        buf[(row_a, row_b)[which]] = summed.astype(BF16)
        for d in range(1, count):
            line(which, d).start()
        for d in range(1, count):
            line(which, d, True).wait_recv()
        summed = buf[0].astype(F32)
        for k in range(1, count):
            summed = summed + buf[k].astype(F32)
    dw_ref[...] = summed
    out_copy.wait()

    for p in range(HALVES):
        for kind in range(4):
            halo(kind, p).wait_send()
        for kind in range(2):
            gm_hop(kind, p).wait_send()
    for b in (0, 1):
        ring_all(b).wait_send()
        for k in range(3):
            cross(b, k).wait_send()
        sib_copy(b).wait_send()
    lp_all().wait_send()
    to_sib_g.wait_send()
    to_sib_l.wait_send()
    for side in (0, 1):
        dwx(side, 0).wait_send()
        dwx(side, 1).wait_send()
        dwx2(side).wait_send()
    dwy_all().wait_send()
    for which in (0, 1):
        for d in range(1, (inner, outer)[which]):
            line(which, d).wait_send()


def hand_over(a_ref, b_ref, out_a, out_b):
    out_a[...] = a_ref[...]
    out_b[...] = b_ref[...]


def shards(mesh_sizes, events, input_weight, output_weight, positives, negatives, log_probs, lengths):
    ndp, nx, nz = mesh_sizes
    ny = ndp // 2
    rows, width = events.shape
    heads = HEADS
    users = lengths.shape[0]
    outer = 3 if nz % 3 == 0 else 1
    inner = nz // outer
    out_rows = width // (ndp * nx)
    piece_rows = rows // (2 * nx)
    events_all = rows * ndp * nx * nz
    lens = lengths.reshape(users // rows, rows)
    lps = log_probs.reshape(1, rows)
    v = pltpu.VMEM
    dma = pltpu.SemaphoreType.DMA
    scratch = [
        v((rows, width), BF16),
        v((4, width, width), BF16),
        v((width, width), BF16),
        v((rows, width), BF16),
        v((rows, width), BF16),
        v((5, rows, width), BF16),
        v((rows, width), F32),
        v((4, rows, width), F32),
        v((rows, width), BF16),
        v((3, rows, width), BF16),
        v((3, rows, width), BF16),
        v((3, rows, width), BF16),
        v((rows, 3 * rows), F32),
        v((rows, 3 * rows), F32),
        v((heads, rows, 3 * rows), F32),
        v((rows, width), F32),
        v((nz, 2 * nx, piece_rows, width), BF16),
        v((nz, 8, rows), F32),
        v((rows, nz * rows), BF16),
        v((rows, width), F32),
        v((rows, width), F32),
        v((2, rows, width), BF16),
        v((2, nx, ny, out_rows, rows), BF16),
        v((nx, ny, out_rows, rows), BF16),
        v((3, rows, width), BF16),
        v((rows, width), F32),
        v((rows, 4 * width), BF16),
        v((rows, width), F32),
        v((rows, width), F32),
        v((rows, width), F32),
        v((2, 2, ny, out_rows, width // 2), BF16),
        v((2, 2, ny, out_rows, width // 2), BF16),
        v((2, ny, out_rows, width // 2), BF16),
        v((2, ny, out_rows, width // 2), BF16),
        v((2, ny, out_rows, width // 2), F32),
        v((ny, out_rows, width), F32),
        v((ny, out_rows, width), BF16),
        v((ny - 1, out_rows, width), BF16),
        v((inner, out_rows, width), BF16),
        v((outer, out_rows, width), BF16),
        dma((9,)),
        dma((4, HALVES)),
        dma((4, HALVES)),
        dma((2, HALVES)),
        dma((2, HALVES)),
        dma((2,)),
        dma((2,)),
        dma((2, 3)),
        dma((2, 3)),
        dma((2,)),
        dma((2,)),
        dma((1,)),
        dma((1,)),
        dma((2,)),
        dma((2,)),
        dma((2, 3)),
        dma((2, 3)),
        dma((1,)),
        dma((1,)),
        dma((inner,)),
        dma((inner,)),
        dma((outer,)),
        dma((outer,)),
    ]
    hbm = pl.BlockSpec(memory_space=pl.ANY)
    vmem = pl.BlockSpec(memory_space=pltpu.VMEM)
    results = pl.pallas_call(
        functools.partial(kernel, (ny, nx, nz, width, heads, events_all)),
        out_shape=(
            jax.ShapeDtypeStruct((rows, width), F32),
            jax.ShapeDtypeStruct((out_rows, width), F32),
        ),
        in_specs=[vmem, vmem, hbm, hbm, hbm, hbm, hbm],
        out_specs=(hbm, vmem),
        scratch_shapes=scratch,
        compiler_params=pltpu.CompilerParams(
            collective_id=0, has_side_effects=True, vmem_limit_bytes=56 * 1024 * 1024
        ),
    )(lens, lps, events, input_weight, output_weight, positives, negatives)
    return pl.pallas_call(
        hand_over,
        out_shape=tuple(jax.ShapeDtypeStruct(r.shape, r.dtype) for r in results),
        in_specs=[vmem, vmem],
        out_specs=(vmem, vmem),
    )(*results)


def solution(mesh):
    sizes = tuple(mesh.shape[a] for a in AXES)
    placed = (
        P(AXES, None),
        P(),
        P(),
        P(AXES, None),
        P("pool", None),
        P("pool"),
        P(),
    )
    return jax.shard_map(
        functools.partial(shards, sizes),
        mesh=mesh,
        in_specs=placed,
        out_specs=(P(AXES, None), P(("dp", "seq"), None)),
        check_vma=False,
    )
```

```python
import functools
import math

import jax
import jax.numpy as jnp
from jax import lax
from jax.experimental import pallas as pl
from jax.experimental.pallas import tpu as pltpu
from jax.sharding import PartitionSpec as P

HEADS = 8
EV_DEV = 128

epsilon = 1e-05
sharpness_divisor = 0.05
loss_multiplier = 8.0

MESH = pl.DeviceIdType.MESH
AXES = ("dp", "seq", "pool")
NT = (((1,), (1,)), ((), ()))
NN = (((1,), (0,)), ((), ()))
HALVES = 2
F32 = jnp.float32
BF16 = jnp.bfloat16


def dot(a, b, dims=NN):
    return lax.dot_general(a, b, dims, preferred_element_type=F32)


def slope(v):
    sg = jax.nn.sigmoid(v)
    return sg * (1.0 + v * (1.0 - sg))


def mean_last(v):
    return jnp.mean(v, axis=1, keepdims=True)


def normalize(row_data):
    centred = row_data - mean_last(row_data)
    inv_std = lax.rsqrt(mean_last(centred * centred) + epsilon)
    return centred * inv_std, inv_std


def norm_back(grad_in, normed, inv_std):
    return (grad_in - mean_last(grad_in) - normed * mean_last(grad_in * normed)) * inv_std


def kernel(
    sizes,
    lens_ref,
    lp_ref,
    ev_hbm,
    win_hbm,
    wout_hbm,
    pos_hbm,
    neg_hbm,
    dev_hbm,
    dw_ref,
    ev,
    win,
    wout,
    pos,
    negs_raw,
    xn,
    normed_x,
    slopes,
    upd,
    qb,
    kb,
    vb,
    mask_f,
    mask_t,
    sc_slope,
    mixed,
    neg,
    lpb,
    ebuf,
    unit,
    gout,
    gl2,
    gt,
    gt_sib,
    gm,
    gact,
    gpre,
    dout,
    gkeys,
    gvals,
    send_a,
    recv_x,
    send_a2,
    recv_x2,
    part_x,
    own_b,
    send_b,
    recv_y,
    line_a,
    line_b,
    load_sem,
    halo_s,
    halo_r,
    gm_s,
    gm_r,
    ring_s,
    ring_r,
    xs_s,
    xs_r,
    sib_s,
    sib_r,
    lp_s,
    lp_r,
    pair_s,
    pair_r,
    dwx_s,
    dwx_r,
    dwy_s,
    dwy_r,
    dwz_s,
    dwz_r,
    fin_s,
    fin_r,
):
    ny, nx, nz, width, heads, events_all = sizes
    hw = width // heads
    rows = EV_DEV
    cb = 256
    inner, outer = line_a.shape[0], line_b.shape[0]
    out_rows = line_a.shape[1]
    scale = 1.0 / math.sqrt(hw)

    dp = lax.axis_index("dp")
    sx = lax.axis_index("seq")
    pz = lax.axis_index("pool")
    core = lax.rem(dp, 2)
    yy = lax.div(dp, 2)
    other = dp + 1 - 2 * core
    total = 2 * ny * nx * nz
    me = (dp * nx + sx) * nz + pz

    def place(i):
        return (lax.div(i, nx * nz), lax.rem(lax.div(i, nz), nx), lax.rem(i, nz))

    nxt = place(lax.rem(me + 1, total))
    prv = place(lax.rem(me + total - 1, total))
    sib = (other, sx, pz)

    xa = sx + 1 - 2 * lax.rem(sx, 2)
    xb = nx - 1 - sx
    dev_a = (dp, xa, pz)
    dev_b = (dp, xb, pz)

    def at_y(d):
        return (lax.rem(yy + d, ny) * 2 + core, sx, pz)

    def at_z(d):
        return (dp, sx, lax.rem(pz + d, nz))

    def load(i, src, dst):
        return pltpu.make_async_copy(src, dst, load_sem.at[i])

    def remote(src, dst, s, r, dev):
        return pltpu.make_async_remote_copy(
            src_ref=src, dst_ref=dst, send_sem=s, recv_sem=r, device_id=dev, device_id_type=MESH
        )

    loads = [
        load(0, neg_hbm, negs_raw),
        load(1, ev_hbm, ev),
        load(2, win_hbm.at[:, pl.ds(2 * width, width)], win.at[2]),
        load(3, win_hbm.at[:, pl.ds(3 * width, width)], win.at[3]),
        load(4, win_hbm.at[:, pl.ds(width, width)], win.at[1]),
        load(5, win_hbm.at[:, pl.ds(0, width)], win.at[0]),
        load(6, wout_hbm, wout),
        load(7, pos_hbm, pos),
    ]
    for item in loads:
        item.start()

    barrier = pltpu.get_barrier_semaphore()
    partners = [nxt, prv, sib]
    partners += [dev_a, dev_b]
    partners += [at_y(d) for d in range(1, ny)]
    partners += [at_z(d) for d in range(1, nz)]
    for partner in partners:
        pl.semaphore_signal(barrier, inc=1, device_id=partner, device_id_type=MESH)

    half = rows // HALVES

    def halo(kind, p):
        a, b, dev = ((2, 1, nxt), (2, 3, prv), (1, 0, nxt), (3, 4, prv))[kind]
        part = pl.ds(p * half, half)
        return remote(
            xn.at[a, part], xn.at[b, part], halo_s.at[kind, p], halo_r.at[kind, p], dev
        )

    def gm_hop(kind, p):
        part = pl.ds(p * half, half)
        return remote(
            gm.at[kind, part], gm.at[kind + 1, part], gm_s.at[kind, p], gm_r.at[kind, p], prv
        )

    colour = lax.rem(sx + 2 * yy, nx)
    piece = core * nx + colour
    hops = sorted(range(1, nz), key=lambda d: (min(d, nz - d), d))
    dev_up = (dp, lax.rem(sx + 1, nx), pz)
    dev_down = (dp, lax.rem(sx + nx - 1, nx), pz)

    near = nz // 2
    batches = (pl.ds(1, near), pl.ds(1 + near, nz - 1 - near))

    def ring(i):
        b = 0 if i < near else 1
        return remote(
            neg.at[0, piece], neg.at[i + 1, piece], ring_s.at[b], ring_r.at[b], at_z(hops[i])
        )

    def ring_all(b):
        ref = neg.at[batches[b], piece]
        return remote(ref, ref, ring_s.at[b], ring_r.at[b], at_z(1))

    def cross(b, k, slot=None):
        ref = neg.at[batches[b], piece if slot is None else slot]
        dev = (dev_up, dev_down, at_y((1, ny - 1)[b]))[k]
        return remote(ref, ref, xs_s.at[b, k], xs_r.at[b, k], dev)

    def cross_arrived(b, k):
        return cross(b, k, core * nx + lax.rem(colour + (3, 1, 2)[k], nx))

    def sib_copy(b):
        ref = neg.at[batches[b], pl.ds(core * nx, nx)]
        return remote(ref, ref, sib_s.at[b], sib_r.at[b], sib)

    def sib_arrived(b):
        ref = neg.at[batches[b], pl.ds((1 - core) * nx, nx)]
        return remote(ref, ref, sib_s.at[b], sib_r.at[b], sib)

    def lp_copy(i):
        return remote(lpb.at[0], lpb.at[i + 1], lp_s.at[0], lp_r.at[0], at_z(hops[i]))

    def lp_all():
        ref = lpb.at[pl.ds(1, nz - 1)]
        return remote(ref, ref, lp_s.at[0], lp_r.at[0], at_z(1))

    loads[0].wait()
    raw = negs_raw[...].astype(F32)
    unit_neg = raw * lax.rsqrt(jnp.sum(raw * raw, axis=1, keepdims=True))
    neg[0] = unit_neg.astype(BF16).reshape(neg.shape[1:])
    lpb[0] = jnp.broadcast_to(lp_ref[...].astype(F32), lpb.shape[1:])
    loads[1].wait()
    own_x, inv_x = normalize(ev[...].astype(F32))
    normed_x[...] = own_x
    xn[2] = own_x.astype(BF16)

    pl.semaphore_wait(barrier, len(partners))

    for p in range(HALVES):
        halo(0, p).start()
        halo(1, p).start()
    for i in range(near):
        ring(i).start()

    def serve(b):
        ring_all(b).wait_recv()
        for k in range(3):
            cross(b, k).start()

    def pass_on(b):
        for k in range(3):
            cross_arrived(b, k).wait_recv()
        sib_copy(b).start()

    def project_own(chunk, dst):
        def body(j, carry):
            cols = pl.ds(pl.multiple_of(j * cb, cb), cb)
            pre = dot(xn[2], win[chunk, :, cols])
            sg = jax.nn.sigmoid(pre)
            slopes[chunk, :, cols] = sg * (1.0 + pre * (1.0 - sg))
            dst[:, cols] = (pre * sg).astype(BF16)
            return carry

        lax.fori_loop(0, width // cb, body, 0)

    def project(slot, chunk, dst):
        def body(j, carry):
            cols = pl.ds(pl.multiple_of(j * cb, cb), cb)
            pre = dot(xn[slot], win[chunk, :, cols])
            dst[:, cols] = (pre * jax.nn.sigmoid(pre)).astype(BF16)
            return carry

        lax.fori_loop(0, width // cb, body, 0)

    loads[2].wait()
    project_own(2, kb.at[2])
    loads[3].wait()
    project_own(3, vb.at[2])

    for p in range(HALVES):
        halo(0, p).wait_recv()
        halo(2, p).start()
        halo(1, p).wait_recv()
        halo(3, p).start()
    for i in range(near, nz - 1):
        ring(i).start()
    for i in range(nz - 1):
        lp_copy(i).start()

    loads[4].wait()
    project_own(1, qb.at[0])
    loads[5].wait()
    project_own(0, upd)

    lens_rows, lens_cols = lens_ref.shape
    users = lens_rows * lens_cols
    lens_line = jnp.concatenate([lens_ref[k : k + 1, :] for k in range(lens_rows)], axis=1)
    lens8 = jnp.broadcast_to(lens_line.astype(F32), (8, users)).astype(BF16)
    ri = lax.broadcasted_iota(jnp.int32, (users, users), 0)
    ci = lax.broadcasted_iota(jnp.int32, (users, users), 1)
    before_cols = (ri < ci).astype(F32).astype(BF16)
    before_rows = (ci < ri).astype(F32).astype(BF16)
    starts_row = dot(lens8, before_cols)[0:1, :]
    starts_col = dot(before_rows, lens8, NT)[:, 0:1]
    first = (me * rows).astype(F32)
    own_pos = first + lax.broadcasted_iota(jnp.int32, (rows, 1), 0).astype(F32)
    own_first = jnp.max(jnp.where(starts_row <= own_pos, starts_row, 0.0), axis=1, keepdims=True)
    key_pos = first - 2.0 * rows + lax.broadcasted_iota(jnp.int32, (rows, 3 * rows), 1).astype(F32)
    mask_f[...] = jnp.where((key_pos >= own_first) & (key_pos <= own_pos), 1.0 / EV_DEV, 0.0)
    row_pos = first + lax.broadcasted_iota(jnp.int32, (1, 3 * rows), 1).astype(F32)
    row_first = jnp.max(jnp.where(starts_col <= row_pos, starts_col, 0.0), axis=0, keepdims=True)
    row_first = jnp.where(row_pos < events_all, row_first, float(2 * events_all))
    mask_t[...] = jnp.where((own_pos >= row_first) & (own_pos <= row_pos), 1.0 / EV_DEV, 0.0)

    project(1, 2, kb.at[1])
    project(1, 3, vb.at[1])
    project(3, 1, qb.at[1])
    serve(0)
    for p in range(HALVES):
        halo(2, p).wait_recv()
    project(0, 2, kb.at[0])
    project(0, 3, vb.at[0])

    def head_forward(h, carry):
        cols = pl.ds(pl.multiple_of(h * hw, hw), hw)
        keys = kb[:, :, cols].reshape(3 * rows, hw)
        values = vb[:, :, cols].reshape(3 * rows, hw)
        s = dot(qb[0, :, cols], keys, NT) * scale
        sg = jax.nn.sigmoid(s)
        seen = mask_f[...]
        sc_slope[h] = seen * (sg * (1.0 + s * (1.0 - sg)))
        w = (s * sg * seen).astype(BF16)
        mixed[:, cols] = dot(w, values)
        return carry

    lax.fori_loop(0, heads // 2, head_forward, 0)
    pass_on(0)
    serve(1)
    lax.fori_loop(heads // 2, heads, head_forward, 0)


    normed_o, inv_o = normalize(mixed[...])
    mixed[...] = normed_o
    gated = normed_o * upd[...].astype(F32)
    gated_low = gated.astype(BF16)
    x_rows = ev[...].astype(F32)
    loads[6].wait()
    layer_out = dot(gated_low, wout[...]) + x_rows
    inv_norm = lax.rsqrt(jnp.sum(layer_out * layer_out, axis=1, keepdims=True))
    unit_out = layer_out * inv_norm
    unit[...] = unit_out
    unit_low = unit_out.astype(BF16)


    per_y = width // ny
    for j in range(ny):
        turned = gated[:, j * per_y : (j + 1) * per_y].T.astype(BF16)
        for c in range(2):
            for k in range(nx):
                r0 = (c * nx + k) * out_rows
                gt[c, k, j] = turned[r0 : r0 + out_rows]
    to_sib_g = remote(gt.at[1 - core], gt_sib, pair_s.at[0], pair_r.at[0], sib)
    to_sib_g.start()

    loads[7].wait()
    pos_rows = pos[...].astype(F32)
    pos_unit = pos_rows * lax.rsqrt(jnp.sum(pos_rows * pos_rows, axis=1, keepdims=True))
    pos_exp = jnp.exp(jnp.sum(unit_out * pos_unit, axis=1, keepdims=True) / sharpness_divisor)

    pass_on(1)
    lp_all().wait_recv()
    def logits(z, exp_total):
        negs = neg[z].reshape(rows, width)
        lg = dot(unit_low, negs, NT) * (1.0 / sharpness_divisor) - lpb[z, 0:1, :]
        e = jnp.exp(lg)
        ebuf[:, pl.ds(pl.multiple_of(z * rows, rows), rows)] = e.astype(BF16)
        return exp_total + jnp.sum(e, axis=1, keepdims=True)

    exp_total = logits(0, jnp.zeros((rows, 1), F32))
    for b, (lo, hi) in enumerate(((1, 1 + near), (1 + near, nz))):
        sib_arrived(b).wait_recv()
        exp_total = lax.fori_loop(lo, hi, logits, exp_total)
    denominator = pos_exp + exp_total
    mixed_negs = dot(ebuf[...], neg[...].reshape(nz * rows, width))
    unit_out = unit[...]
    grad_unit = (
        loss_multiplier
        / sharpness_divisor
        * (mixed_negs / denominator + (pos_exp / denominator - 1.0) * pos_unit)
    )
    grad_out = (
        grad_unit - unit_out * jnp.sum(unit_out * grad_unit, axis=1, keepdims=True)
    ) * inv_norm
    gout[...] = grad_out
    gl2[0] = grad_out.astype(BF16)
    to_sib_l = remote(gl2.at[0], gl2.at[1], pair_s.at[1], pair_r.at[1], sib)
    to_sib_l.start()

    def gate_back(j, carry):
        cols = pl.ds(pl.multiple_of(j * cb, cb), cb)
        gact[:, cols] = dot(gl2[0], wout[cols, :], NT)
        return carry

    lax.fori_loop(0, width // cb, gate_back, 0)
    grad_gated = gact[...]
    normed_o = mixed[...]
    gpre[:, 0:width] = (grad_gated * normed_o * slopes[0]).astype(BF16)
    gm[0] = norm_back(grad_gated * upd[...].astype(F32), normed_o, inv_o).astype(BF16)
    for p in range(HALVES):
        gm_hop(0, p).start()

    to_sib_g.wait_recv()
    to_sib_l.wait_recv()

    def weight_part(k):
        mine = gt[core, k].reshape(ny * out_rows, rows)
        theirs = gt_sib[k].reshape(ny * out_rows, rows)
        left = jnp.concatenate([mine, theirs], axis=1)
        return dot(left, gl2[...].reshape(2 * rows, width))

    wide = width // 2

    def dwx(side, i):
        return remote(
            send_a.at[side, i], recv_x.at[side, i], dwx_s.at[side, i], dwx_r.at[side, i], (dev_a, dev_b)[side]
        )

    def dwx2(side):
        return remote(
            send_a2.at[side], recv_x2.at[side], dwx_s.at[side, 2], dwx_r.at[side, 2], (dev_b, dev_a)[side]
        )

    part = weight_part(lax.rem(sx + 2, nx))
    for side in (0, 1):
        send_a[side, 0] = part[:, side * wide : (side + 1) * wide].astype(BF16).reshape(send_a.shape[2:])
        dwx(side, 0).start()
    for side, at in ((0, xa), (1, xb)):
        part = weight_part(at)
        send_a[side, 1] = part[:, side * wide : (side + 1) * wide].astype(BF16).reshape(send_a.shape[2:])
        dwx(side, 1).start()
        part_x[1 - side] = part[:, (1 - side) * wide : (2 - side) * wide].reshape(part_x.shape[1:])
    own_b[...] = weight_part(sx).reshape(own_b.shape)

    def head_query(h, carry):
        cols = pl.ds(pl.multiple_of(h * hw, hw), hw)
        values = vb[:, :, cols].reshape(3 * rows, hw)
        keys = kb[:, :, cols].reshape(3 * rows, hw)
        gs = (dot(gm[0, :, cols], values, NT) * sc_slope[h]).astype(BF16)
        gq = dot(gs, keys) * scale
        at = pl.ds(pl.multiple_of(width + h * hw, hw), hw)
        gpre[:, at] = (gq * slopes[1, :, cols]).astype(BF16)
        return carry

    lax.fori_loop(0, heads, head_query, 0)

    for p in range(HALVES):
        gm_hop(0, p).wait_recv()
        gm_hop(1, p).start()

    def dwy(d):
        return remote(
            send_b.at[lax.rem(yy + d, ny)], recv_y.at[d - 1], dwy_s.at[0], dwy_r.at[0], at_y(d)
        )

    def dwy_all():
        return remote(recv_y, recv_y, dwy_s.at[0], dwy_r.at[0], at_y(1))

    def head_keys(lo, count):
        def body(h, carry):
            cols = pl.ds(pl.multiple_of(h * hw, hw), hw)
            queries = qb[lo : lo + count, :, cols].reshape(count * rows, hw)
            grads = gm[lo : lo + count, :, cols].reshape(count * rows, hw)
            s = dot(kb[2, :, cols], queries, NT) * scale
            sg = jax.nn.sigmoid(s)
            seen = mask_t[:, lo * rows : (lo + count) * rows]
            w = (s * sg * seen).astype(BF16)
            gv = dot(w, grads)
            gs = (dot(vb[2, :, cols], grads, NT) * seen * (sg * (1.0 + s * (1.0 - sg)))).astype(BF16)
            gk = dot(gs, queries)
            if lo == 0:
                gvals[:, cols] = gv
                gkeys[:, cols] = gk
                return carry
            gv = gv + gvals[:, cols]
            gk = (gk + gkeys[:, cols]) * scale
            at = pl.ds(pl.multiple_of(2 * width + h * hw, hw), hw)
            gpre[:, at] = (gk * slopes[2, :, cols]).astype(BF16)
            at = pl.ds(pl.multiple_of(3 * width + h * hw, hw), hw)
            gpre[:, at] = (gv * slopes[3, :, cols]).astype(BF16)
            return carry

        lax.fori_loop(0, heads, body, 0)

    head_keys(0, 2)

    for side in (0, 1):
        dwx(side, 0).wait_recv()
        send_a2[side] = (part_x[side] + recv_x[side, 0].astype(F32)).astype(BF16)
        dwx2(side).start()

    for p in range(HALVES):
        halo(3, p).wait_recv()
    project(4, 1, qb.at[2])
    for p in range(HALVES):
        gm_hop(1, p).wait_recv()
    head_keys(2, 1)

    for side in (0, 1):
        dwx(side, 1).wait_recv()
        dwx2(side).wait_recv()
        half_cols = pl.ds(side * wide, wide)
        summed = own_b[:, :, half_cols] + recv_x[side, 1].astype(F32) + recv_x2[side].astype(F32)
        own_b[:, :, half_cols] = summed
        send_b[:, :, half_cols] = summed.astype(BF16)
    for d in range(1, ny):
        dwy(d).start()

    def x_back(j, carry):
        cols = pl.ds(pl.multiple_of(j * cb, cb), cb)
        part = dot(gpre[:, 0:width], win[0, cols, :], NT)
        for c in range(1, 4):
            part = part + dot(gpre[:, c * width : (c + 1) * width], win[c, cols, :], NT)
        gact[:, cols] = part
        return carry

    lax.fori_loop(0, width // cb, x_back, 0)
    dout[...] = norm_back(gact[...], normed_x[...], inv_x) + gout[...]
    out_copy = pltpu.make_async_copy(dout, dev_hbm, load_sem.at[8])
    out_copy.start()

    row_a, row_b = lax.rem(pz, inner), lax.div(pz, inner)

    def line(which, d, source=False):
        count = (inner, outer)[which]
        spot = (row_a, row_b)[which]
        there = lax.rem(spot + (count - d if source else d), count)
        to = lax.rem(spot + d, count)
        buf = (line_a, line_b)[which]
        ref = buf.at[there if source else spot]
        dev = (dp, sx, row_b * inner + to) if which == 0 else (dp, sx, to * inner + row_a)
        return remote(ref, ref, (dwz_s, fin_s)[which].at[d - 1], (dwz_r, fin_r)[which].at[d - 1], dev)

    dwy_all().wait_recv()
    summed = own_b[yy]
    for d in range(1, ny):
        summed = summed + recv_y[d - 1].astype(F32)
    for which in (0, 1):
        buf, count = ((line_a, inner), (line_b, outer))[which]
        buf[(row_a, row_b)[which]] = summed.astype(BF16)
        for d in range(1, count):
            line(which, d).start()
        for d in range(1, count):
            line(which, d, True).wait_recv()
        summed = buf[0].astype(F32)
        for k in range(1, count):
            summed = summed + buf[k].astype(F32)
    dw_ref[...] = summed
    out_copy.wait()

    for p in range(HALVES):
        for kind in range(4):
            halo(kind, p).wait_send()
        for kind in range(2):
            gm_hop(kind, p).wait_send()
    for b in (0, 1):
        ring_all(b).wait_send()
        for k in range(3):
            cross(b, k).wait_send()
        sib_copy(b).wait_send()
    lp_all().wait_send()
    to_sib_g.wait_send()
    to_sib_l.wait_send()
    for side in (0, 1):
        dwx(side, 0).wait_send()
        dwx(side, 1).wait_send()
        dwx2(side).wait_send()
    dwy_all().wait_send()
    for which in (0, 1):
        for d in range(1, (inner, outer)[which]):
            line(which, d).wait_send()


def hand_over(a_ref, b_ref, out_a, out_b):
    out_a[...] = a_ref[...]
    out_b[...] = b_ref[...]


def shards(mesh_sizes, events, input_weight, output_weight, positives, negatives, log_probs, lengths):
    ndp, nx, nz = mesh_sizes
    ny = ndp // 2
    rows, width = events.shape
    heads = HEADS
    users = lengths.shape[0]
    outer = 3 if nz % 3 == 0 else 1
    inner = nz // outer
    out_rows = width // (ndp * nx)
    piece_rows = rows // (2 * nx)
    events_all = rows * ndp * nx * nz
    lens = lengths.reshape(users // rows, rows)
    lps = log_probs.reshape(1, rows)
    v = pltpu.VMEM
    dma = pltpu.SemaphoreType.DMA
    scratch = [
        v((rows, width), BF16),
        v((4, width, width), BF16),
        v((width, width), BF16),
        v((rows, width), BF16),
        v((rows, width), BF16),
        v((5, rows, width), BF16),
        v((rows, width), F32),
        v((4, rows, width), F32),
        v((rows, width), BF16),
        v((3, rows, width), BF16),
        v((3, rows, width), BF16),
        v((3, rows, width), BF16),
        v((rows, 3 * rows), F32),
        v((rows, 3 * rows), F32),
        v((heads, rows, 3 * rows), F32),
        v((rows, width), F32),
        v((nz, 2 * nx, piece_rows, width), BF16),
        v((nz, 8, rows), F32),
        v((rows, nz * rows), BF16),
        v((rows, width), F32),
        v((rows, width), F32),
        v((2, rows, width), BF16),
        v((2, nx, ny, out_rows, rows), BF16),
        v((nx, ny, out_rows, rows), BF16),
        v((3, rows, width), BF16),
        v((rows, width), F32),
        v((rows, 4 * width), BF16),
        v((rows, width), F32),
        v((rows, width), F32),
        v((rows, width), F32),
        v((2, 2, ny, out_rows, width // 2), BF16),
        v((2, 2, ny, out_rows, width // 2), BF16),
        v((2, ny, out_rows, width // 2), BF16),
        v((2, ny, out_rows, width // 2), BF16),
        v((2, ny, out_rows, width // 2), F32),
        v((ny, out_rows, width), F32),
        v((ny, out_rows, width), BF16),
        v((ny - 1, out_rows, width), BF16),
        v((inner, out_rows, width), BF16),
        v((outer, out_rows, width), BF16),
        dma((9,)),
        dma((4, HALVES)),
        dma((4, HALVES)),
        dma((2, HALVES)),
        dma((2, HALVES)),
        dma((2,)),
        dma((2,)),
        dma((2, 3)),
        dma((2, 3)),
        dma((2,)),
        dma((2,)),
        dma((1,)),
        dma((1,)),
        dma((2,)),
        dma((2,)),
        dma((2, 3)),
        dma((2, 3)),
        dma((1,)),
        dma((1,)),
        dma((inner,)),
        dma((inner,)),
        dma((outer,)),
        dma((outer,)),
    ]
    hbm = pl.BlockSpec(memory_space=pl.ANY)
    vmem = pl.BlockSpec(memory_space=pltpu.VMEM)
    results = pl.pallas_call(
        functools.partial(kernel, (ny, nx, nz, width, heads, events_all)),
        out_shape=(
            jax.ShapeDtypeStruct((rows, width), F32),
            jax.ShapeDtypeStruct((out_rows, width), F32),
        ),
        in_specs=[vmem, vmem, hbm, hbm, hbm, hbm, hbm],
        out_specs=(hbm, vmem),
        scratch_shapes=scratch,
        compiler_params=pltpu.CompilerParams(
            collective_id=0, has_side_effects=True, vmem_limit_bytes=56 * 1024 * 1024
        ),
    )(lens, lps, events, input_weight, output_weight, positives, negatives)
    return pl.pallas_call(
        hand_over,
        out_shape=tuple(jax.ShapeDtypeStruct(r.shape, r.dtype) for r in results),
        in_specs=[vmem, vmem],
        out_specs=(vmem, vmem),
    )(*results)


def solution(mesh):
    sizes = tuple(mesh.shape[a] for a in AXES)
    placed = (
        P(AXES, None),
        P(),
        P(),
        P(AXES, None),
        P("pool", None),
        P("pool"),
        P(),
    )
    return jax.shard_map(
        functools.partial(shards, sizes),
        mesh=mesh,
        in_specs=placed,
        out_specs=(P(AXES, None), P(("dp", "seq"), None)),
        check_vma=False,
    )
```

```python
import functools
import math

import jax
import jax.numpy as jnp
from jax import lax
from jax.experimental import pallas as pl
from jax.experimental.pallas import tpu as pltpu
from jax.sharding import PartitionSpec as P

HEADS = 8
EV_DEV = 128

epsilon = 1e-05
sharpness_divisor = 0.05
loss_multiplier = 8.0

MESH = pl.DeviceIdType.MESH
AXES = ("dp", "seq", "pool")
NT = (((1,), (1,)), ((), ()))
NN = (((1,), (0,)), ((), ()))
HALVES = 2
F32 = jnp.float32
BF16 = jnp.bfloat16


def dot(a, b, dims=NN):
    return lax.dot_general(a, b, dims, preferred_element_type=F32)


def slope(v):
    sg = jax.nn.sigmoid(v)
    return sg * (1.0 + v * (1.0 - sg))


def mean_last(v):
    return jnp.mean(v, axis=1, keepdims=True)


def normalize(row_data):
    centred = row_data - mean_last(row_data)
    inv_std = lax.rsqrt(mean_last(centred * centred) + epsilon)
    return centred * inv_std, inv_std


def norm_back(grad_in, normed, inv_std):
    return (grad_in - mean_last(grad_in) - normed * mean_last(grad_in * normed)) * inv_std


def kernel(
    sizes,
    lens_ref,
    lp_ref,
    ev_hbm,
    win_hbm,
    wout_hbm,
    pos_hbm,
    neg_hbm,
    dev_hbm,
    dw_ref,
    ev,
    win,
    wout,
    pos,
    negs_raw,
    xn,
    normed_x,
    slopes,
    upd,
    qb,
    kb,
    vb,
    mask_f,
    mask_t,
    sc_slope,
    mixed,
    neg,
    lpb,
    ebuf,
    unit,
    gout,
    gl2,
    gt,
    gt_sib,
    gm,
    gact,
    gpre,
    dout,
    gkeys,
    gvals,
    send_a,
    recv_x,
    send_a2,
    recv_x2,
    part_x,
    own_b,
    send_b,
    recv_y,
    line_a,
    line_b,
    load_sem,
    halo_s,
    halo_r,
    gm_s,
    gm_r,
    ring_s,
    ring_r,
    xs_s,
    xs_r,
    sib_s,
    sib_r,
    lp_s,
    lp_r,
    pair_s,
    pair_r,
    dwx_s,
    dwx_r,
    dwy_s,
    dwy_r,
    dwz_s,
    dwz_r,
    fin_s,
    fin_r,
):
    ny, nx, nz, width, heads, events_all = sizes
    hw = width // heads
    rows = EV_DEV
    cb = 256
    inner, outer = line_a.shape[0], line_b.shape[0]
    out_rows = line_a.shape[1]
    scale = 1.0 / math.sqrt(hw)

    dp = lax.axis_index("dp")
    sx = lax.axis_index("seq")
    pz = lax.axis_index("pool")
    core = lax.rem(dp, 2)
    yy = lax.div(dp, 2)
    other = dp + 1 - 2 * core
    total = 2 * ny * nx * nz
    me = (dp * nx + sx) * nz + pz

    def place(i):
        return (lax.div(i, nx * nz), lax.rem(lax.div(i, nz), nx), lax.rem(i, nz))

    nxt = place(lax.rem(me + 1, total))
    prv = place(lax.rem(me + total - 1, total))
    sib = (other, sx, pz)

    xa = sx + 1 - 2 * lax.rem(sx, 2)
    xb = nx - 1 - sx
    dev_a = (dp, xa, pz)
    dev_b = (dp, xb, pz)

    def at_y(d):
        return (lax.rem(yy + d, ny) * 2 + core, sx, pz)

    def at_z(d):
        return (dp, sx, lax.rem(pz + d, nz))

    def load(i, src, dst):
        return pltpu.make_async_copy(src, dst, load_sem.at[i])

    def remote(src, dst, s, r, dev):
        return pltpu.make_async_remote_copy(
            src_ref=src, dst_ref=dst, send_sem=s, recv_sem=r, device_id=dev, device_id_type=MESH
        )

    loads = [
        load(0, neg_hbm, negs_raw),
        load(1, ev_hbm, ev),
        load(2, win_hbm.at[:, pl.ds(2 * width, width)], win.at[2]),
        load(3, win_hbm.at[:, pl.ds(3 * width, width)], win.at[3]),
        load(4, win_hbm.at[:, pl.ds(width, width)], win.at[1]),
        load(5, win_hbm.at[:, pl.ds(0, width)], win.at[0]),
        load(6, wout_hbm, wout),
        load(7, pos_hbm, pos),
    ]
    for item in loads:
        item.start()

    barrier = pltpu.get_barrier_semaphore()
    partners = [nxt, prv, sib]
    partners += [dev_a, dev_b]
    partners += [at_y(d) for d in range(1, ny)]
    partners += [at_z(d) for d in range(1, nz)]
    for partner in partners:
        pl.semaphore_signal(barrier, inc=1, device_id=partner, device_id_type=MESH)

    half = rows // HALVES

    def halo(kind, p):
        a, b, dev = ((2, 1, nxt), (2, 3, prv), (1, 0, nxt), (3, 4, prv))[kind]
        part = pl.ds(p * half, half)
        return remote(
            xn.at[a, part], xn.at[b, part], halo_s.at[kind, p], halo_r.at[kind, p], dev
        )

    def gm_hop(kind, p):
        part = pl.ds(p * half, half)
        return remote(
            gm.at[kind, part], gm.at[kind + 1, part], gm_s.at[kind, p], gm_r.at[kind, p], prv
        )

    colour = lax.rem(sx + 2 * yy, nx)
    piece = core * nx + colour
    hops = sorted(range(1, nz), key=lambda d: (min(d, nz - d), d))
    dev_up = (dp, lax.rem(sx + 1, nx), pz)
    dev_down = (dp, lax.rem(sx + nx - 1, nx), pz)

    near = nz // 2
    batches = (pl.ds(1, near), pl.ds(1 + near, nz - 1 - near))

    def ring(i):
        b = 0 if i < near else 1
        return remote(
            neg.at[0, piece], neg.at[i + 1, piece], ring_s.at[b], ring_r.at[b], at_z(hops[i])
        )

    def ring_all(b):
        ref = neg.at[batches[b], piece]
        return remote(ref, ref, ring_s.at[b], ring_r.at[b], at_z(1))

    def cross(b, k, slot=None):
        ref = neg.at[batches[b], piece if slot is None else slot]
        dev = (dev_up, dev_down, at_y((1, ny - 1)[b]))[k]
        return remote(ref, ref, xs_s.at[b, k], xs_r.at[b, k], dev)

    def cross_arrived(b, k):
        return cross(b, k, core * nx + lax.rem(colour + (3, 1, 2)[k], nx))

    def sib_copy(b):
        ref = neg.at[batches[b], pl.ds(core * nx, nx)]
        return remote(ref, ref, sib_s.at[b], sib_r.at[b], sib)

    def sib_arrived(b):
        ref = neg.at[batches[b], pl.ds((1 - core) * nx, nx)]
        return remote(ref, ref, sib_s.at[b], sib_r.at[b], sib)

    def lp_copy(i):
        return remote(lpb.at[0], lpb.at[i + 1], lp_s.at[0], lp_r.at[0], at_z(hops[i]))

    def lp_all():
        ref = lpb.at[pl.ds(1, nz - 1)]
        return remote(ref, ref, lp_s.at[0], lp_r.at[0], at_z(1))

    loads[0].wait()
    raw = negs_raw[...].astype(F32)
    unit_neg = raw * lax.rsqrt(jnp.sum(raw * raw, axis=1, keepdims=True))
    neg[0] = unit_neg.astype(BF16).reshape(neg.shape[1:])
    lpb[0] = jnp.broadcast_to(lp_ref[...].astype(F32), lpb.shape[1:])
    loads[1].wait()
    own_x, inv_x = normalize(ev[...].astype(F32))
    normed_x[...] = own_x
    xn[2] = own_x.astype(BF16)

    pl.semaphore_wait(barrier, len(partners))

    for p in range(HALVES):
        halo(0, p).start()
        halo(1, p).start()
    for i in range(near):
        ring(i).start()

    def serve(b):
        ring_all(b).wait_recv()
        for k in range(3):
            cross(b, k).start()

    def pass_on(b):
        for k in range(3):
            cross_arrived(b, k).wait_recv()
        sib_copy(b).start()

    def project_own(chunk, dst):
        def body(j, carry):
            cols = pl.ds(pl.multiple_of(j * cb, cb), cb)
            pre = dot(xn[2], win[chunk, :, cols])
            sg = jax.nn.sigmoid(pre)
            slopes[chunk, :, cols] = sg * (1.0 + pre * (1.0 - sg))
            dst[:, cols] = (pre * sg).astype(BF16)
            return carry

        lax.fori_loop(0, width // cb, body, 0)

    def project(slot, chunk, dst):
        def body(j, carry):
            cols = pl.ds(pl.multiple_of(j * cb, cb), cb)
            pre = dot(xn[slot], win[chunk, :, cols])
            dst[:, cols] = (pre * jax.nn.sigmoid(pre)).astype(BF16)
            return carry

        lax.fori_loop(0, width // cb, body, 0)

    loads[2].wait()
    project_own(2, kb.at[2])
    loads[3].wait()
    project_own(3, vb.at[2])

    for p in range(HALVES):
        halo(0, p).wait_recv()
        halo(2, p).start()
        halo(1, p).wait_recv()
        halo(3, p).start()
    for i in range(near, nz - 1):
        ring(i).start()
    for i in range(nz - 1):
        lp_copy(i).start()

    loads[4].wait()
    project_own(1, qb.at[0])
    loads[5].wait()
    project_own(0, upd)

    lens_rows, lens_cols = lens_ref.shape
    users = lens_rows * lens_cols
    lens_line = jnp.concatenate([lens_ref[k : k + 1, :] for k in range(lens_rows)], axis=1)
    lens8 = jnp.broadcast_to(lens_line.astype(F32), (8, users)).astype(BF16)
    ri = lax.broadcasted_iota(jnp.int32, (users, users), 0)
    ci = lax.broadcasted_iota(jnp.int32, (users, users), 1)
    before_cols = (ri < ci).astype(F32).astype(BF16)
    before_rows = (ci < ri).astype(F32).astype(BF16)
    starts_row = dot(lens8, before_cols)[0:1, :]
    starts_col = dot(before_rows, lens8, NT)[:, 0:1]
    first = (me * rows).astype(F32)
    own_pos = first + lax.broadcasted_iota(jnp.int32, (rows, 1), 0).astype(F32)
    own_first = jnp.max(jnp.where(starts_row <= own_pos, starts_row, 0.0), axis=1, keepdims=True)
    key_pos = first - 2.0 * rows + lax.broadcasted_iota(jnp.int32, (rows, 3 * rows), 1).astype(F32)
    mask_f[...] = jnp.where((key_pos >= own_first) & (key_pos <= own_pos), 1.0 / EV_DEV, 0.0)
    row_pos = first + lax.broadcasted_iota(jnp.int32, (1, 3 * rows), 1).astype(F32)
    row_first = jnp.max(jnp.where(starts_col <= row_pos, starts_col, 0.0), axis=0, keepdims=True)
    row_first = jnp.where(row_pos < events_all, row_first, float(2 * events_all))
    mask_t[...] = jnp.where((own_pos >= row_first) & (own_pos <= row_pos), 1.0 / EV_DEV, 0.0)

    project(1, 2, kb.at[1])
    project(1, 3, vb.at[1])
    project(3, 1, qb.at[1])
    serve(0)
    for p in range(HALVES):
        halo(2, p).wait_recv()
    project(0, 2, kb.at[0])
    project(0, 3, vb.at[0])

    def head_forward(h, carry):
        cols = pl.ds(pl.multiple_of(h * hw, hw), hw)
        keys = kb[:, :, cols].reshape(3 * rows, hw)
        values = vb[:, :, cols].reshape(3 * rows, hw)
        s = dot(qb[0, :, cols], keys, NT) * scale
        sg = jax.nn.sigmoid(s)
        seen = mask_f[...]
        sc_slope[h] = seen * (sg * (1.0 + s * (1.0 - sg)))
        w = (s * sg * seen).astype(BF16)
        mixed[:, cols] = dot(w, values)
        return carry

    lax.fori_loop(0, heads // 2, head_forward, 0, unroll=2)
    pass_on(0)
    serve(1)
    lax.fori_loop(heads // 2, heads, head_forward, 0, unroll=2)


    normed_o, inv_o = normalize(mixed[...])
    mixed[...] = normed_o
    gated = normed_o * upd[...].astype(F32)
    gated_low = gated.astype(BF16)
    x_rows = ev[...].astype(F32)
    loads[6].wait()
    layer_out = dot(gated_low, wout[...]) + x_rows
    inv_norm = lax.rsqrt(jnp.sum(layer_out * layer_out, axis=1, keepdims=True))
    unit_out = layer_out * inv_norm
    unit[...] = unit_out
    unit_low = unit_out.astype(BF16)


    per_y = width // ny
    for j in range(ny):
        turned = gated[:, j * per_y : (j + 1) * per_y].T.astype(BF16)
        for c in range(2):
            for k in range(nx):
                r0 = (c * nx + k) * out_rows
                gt[c, k, j] = turned[r0 : r0 + out_rows]
    to_sib_g = remote(gt.at[1 - core], gt_sib, pair_s.at[0], pair_r.at[0], sib)
    to_sib_g.start()

    loads[7].wait()
    pos_rows = pos[...].astype(F32)
    pos_unit = pos_rows * lax.rsqrt(jnp.sum(pos_rows * pos_rows, axis=1, keepdims=True))
    pos_exp = jnp.exp(jnp.sum(unit_out * pos_unit, axis=1, keepdims=True) / sharpness_divisor)

    pass_on(1)
    lp_all().wait_recv()
    def logits(z, exp_total):
        negs = neg[z].reshape(rows, width)
        lg = dot(unit_low, negs, NT) * (1.0 / sharpness_divisor) - lpb[z, 0:1, :]
        e = jnp.exp(lg)
        ebuf[:, pl.ds(pl.multiple_of(z * rows, rows), rows)] = e.astype(BF16)
        return exp_total + jnp.sum(e, axis=1, keepdims=True)

    exp_total = logits(0, jnp.zeros((rows, 1), F32))
    for b, (lo, hi) in enumerate(((1, 1 + near), (1 + near, nz))):
        sib_arrived(b).wait_recv()
        exp_total = lax.fori_loop(lo, hi, logits, exp_total)
    denominator = pos_exp + exp_total
    mixed_negs = dot(ebuf[...], neg[...].reshape(nz * rows, width))
    unit_out = unit[...]
    grad_unit = (
        loss_multiplier
        / sharpness_divisor
        * (mixed_negs / denominator + (pos_exp / denominator - 1.0) * pos_unit)
    )
    grad_out = (
        grad_unit - unit_out * jnp.sum(unit_out * grad_unit, axis=1, keepdims=True)
    ) * inv_norm
    gout[...] = grad_out
    gl2[0] = grad_out.astype(BF16)
    to_sib_l = remote(gl2.at[0], gl2.at[1], pair_s.at[1], pair_r.at[1], sib)
    to_sib_l.start()

    def gate_back(j, carry):
        cols = pl.ds(pl.multiple_of(j * cb, cb), cb)
        gact[:, cols] = dot(gl2[0], wout[cols, :], NT)
        return carry

    lax.fori_loop(0, width // cb, gate_back, 0)
    to_sib_g.wait_recv()
    to_sib_l.wait_recv()

    def weight_part(k):
        mine = gt[core, k].reshape(ny * out_rows, rows)
        theirs = gt_sib[k].reshape(ny * out_rows, rows)
        left = jnp.concatenate([mine, theirs], axis=1)
        return dot(left, gl2[...].reshape(2 * rows, width))

    wide = width // 2

    def dwx(side, i):
        return remote(
            send_a.at[side, i], recv_x.at[side, i], dwx_s.at[side, i], dwx_r.at[side, i], (dev_a, dev_b)[side]
        )

    def dwx2(side):
        return remote(
            send_a2.at[side], recv_x2.at[side], dwx_s.at[side, 2], dwx_r.at[side, 2], (dev_b, dev_a)[side]
        )

    part = weight_part(lax.rem(sx + 2, nx))
    for side in (0, 1):
        send_a[side, 0] = part[:, side * wide : (side + 1) * wide].astype(BF16).reshape(send_a.shape[2:])
        dwx(side, 0).start()
    for side, at in ((0, xa), (1, xb)):
        part = weight_part(at)
        send_a[side, 1] = part[:, side * wide : (side + 1) * wide].astype(BF16).reshape(send_a.shape[2:])
        dwx(side, 1).start()
        part_x[1 - side] = part[:, (1 - side) * wide : (2 - side) * wide].reshape(part_x.shape[1:])
    grad_gated = gact[...]
    normed_o = mixed[...]
    gpre[:, 0:width] = (grad_gated * normed_o * slopes[0]).astype(BF16)
    gm[0] = norm_back(grad_gated * upd[...].astype(F32), normed_o, inv_o).astype(BF16)
    for p in range(HALVES):
        gm_hop(0, p).start()

    own_b[...] = weight_part(sx).reshape(own_b.shape)

    def head_query(h, carry):
        cols = pl.ds(pl.multiple_of(h * hw, hw), hw)
        values = vb[:, :, cols].reshape(3 * rows, hw)
        keys = kb[:, :, cols].reshape(3 * rows, hw)
        gs = (dot(gm[0, :, cols], values, NT) * sc_slope[h]).astype(BF16)
        gq = dot(gs, keys) * scale
        at = pl.ds(pl.multiple_of(width + h * hw, hw), hw)
        gpre[:, at] = (gq * slopes[1, :, cols]).astype(BF16)
        return carry

    lax.fori_loop(0, heads, head_query, 0, unroll=2)

    for p in range(HALVES):
        gm_hop(0, p).wait_recv()
        gm_hop(1, p).start()

    def dwy(d):
        return remote(
            send_b.at[lax.rem(yy + d, ny)], recv_y.at[d - 1], dwy_s.at[0], dwy_r.at[0], at_y(d)
        )

    def dwy_all():
        return remote(recv_y, recv_y, dwy_s.at[0], dwy_r.at[0], at_y(1))

    def head_keys(lo, count):
        def body(h, carry):
            cols = pl.ds(pl.multiple_of(h * hw, hw), hw)
            queries = qb[lo : lo + count, :, cols].reshape(count * rows, hw)
            grads = gm[lo : lo + count, :, cols].reshape(count * rows, hw)
            s = dot(kb[2, :, cols], queries, NT) * scale
            sg = jax.nn.sigmoid(s)
            seen = mask_t[:, lo * rows : (lo + count) * rows]
            w = (s * sg * seen).astype(BF16)
            gv = dot(w, grads)
            gs = (dot(vb[2, :, cols], grads, NT) * seen * (sg * (1.0 + s * (1.0 - sg)))).astype(BF16)
            gk = dot(gs, queries)
            if lo == 0:
                gvals[:, cols] = gv
                gkeys[:, cols] = gk
                return carry
            gv = gv + gvals[:, cols]
            gk = (gk + gkeys[:, cols]) * scale
            at = pl.ds(pl.multiple_of(2 * width + h * hw, hw), hw)
            gpre[:, at] = (gk * slopes[2, :, cols]).astype(BF16)
            at = pl.ds(pl.multiple_of(3 * width + h * hw, hw), hw)
            gpre[:, at] = (gv * slopes[3, :, cols]).astype(BF16)
            return carry

        lax.fori_loop(0, heads, body, 0, unroll=2)

    head_keys(0, 2)

    for side in (0, 1):
        dwx(side, 0).wait_recv()
        send_a2[side] = (part_x[side] + recv_x[side, 0].astype(F32)).astype(BF16)
        dwx2(side).start()

    for p in range(HALVES):
        halo(3, p).wait_recv()
    project(4, 1, qb.at[2])
    for p in range(HALVES):
        gm_hop(1, p).wait_recv()
    head_keys(2, 1)

    for side in (0, 1):
        dwx(side, 1).wait_recv()
        dwx2(side).wait_recv()
        half_cols = pl.ds(side * wide, wide)
        summed = own_b[:, :, half_cols] + recv_x[side, 1].astype(F32) + recv_x2[side].astype(F32)
        own_b[:, :, half_cols] = summed
        send_b[:, :, half_cols] = summed.astype(BF16)
    for d in range(1, ny):
        dwy(d).start()

    def x_back(j, carry):
        cols = pl.ds(pl.multiple_of(j * cb, cb), cb)
        part = dot(gpre[:, 0:width], win[0, cols, :], NT)
        for c in range(1, 4):
            part = part + dot(gpre[:, c * width : (c + 1) * width], win[c, cols, :], NT)
        gact[:, cols] = part
        return carry

    lax.fori_loop(0, width // cb, x_back, 0)
    dout[...] = norm_back(gact[...], normed_x[...], inv_x) + gout[...]
    out_copy = pltpu.make_async_copy(dout, dev_hbm, load_sem.at[8])
    out_copy.start()

    row_a, row_b = lax.rem(pz, inner), lax.div(pz, inner)

    def line(which, d, source=False):
        count = (inner, outer)[which]
        spot = (row_a, row_b)[which]
        there = lax.rem(spot + (count - d if source else d), count)
        to = lax.rem(spot + d, count)
        buf = (line_a, line_b)[which]
        ref = buf.at[there if source else spot]
        dev = (dp, sx, row_b * inner + to) if which == 0 else (dp, sx, to * inner + row_a)
        return remote(ref, ref, (dwz_s, fin_s)[which].at[d - 1], (dwz_r, fin_r)[which].at[d - 1], dev)

    dwy_all().wait_recv()
    summed = own_b[yy]
    for d in range(1, ny):
        summed = summed + recv_y[d - 1].astype(F32)
    for which in (0, 1):
        buf, count = ((line_a, inner), (line_b, outer))[which]
        buf[(row_a, row_b)[which]] = summed.astype(BF16)
        for d in range(1, count):
            line(which, d).start()
        for d in range(1, count):
            line(which, d, True).wait_recv()
        summed = buf[0].astype(F32)
        for k in range(1, count):
            summed = summed + buf[k].astype(F32)
    dw_ref[...] = summed
    out_copy.wait()

    for p in range(HALVES):
        for kind in range(4):
            halo(kind, p).wait_send()
        for kind in range(2):
            gm_hop(kind, p).wait_send()
    for b in (0, 1):
        ring_all(b).wait_send()
        for k in range(3):
            cross(b, k).wait_send()
        sib_copy(b).wait_send()
    lp_all().wait_send()
    to_sib_g.wait_send()
    to_sib_l.wait_send()
    for side in (0, 1):
        dwx(side, 0).wait_send()
        dwx(side, 1).wait_send()
        dwx2(side).wait_send()
    dwy_all().wait_send()
    for which in (0, 1):
        for d in range(1, (inner, outer)[which]):
            line(which, d).wait_send()


def hand_over(a_ref, b_ref, out_a, out_b):
    out_a[...] = a_ref[...]
    out_b[...] = b_ref[...]


def shards(mesh_sizes, events, input_weight, output_weight, positives, negatives, log_probs, lengths):
    ndp, nx, nz = mesh_sizes
    ny = ndp // 2
    rows, width = events.shape
    heads = HEADS
    users = lengths.shape[0]
    outer = 3 if nz % 3 == 0 else 1
    inner = nz // outer
    out_rows = width // (ndp * nx)
    piece_rows = rows // (2 * nx)
    events_all = rows * ndp * nx * nz
    lens = lengths.reshape(users // rows, rows)
    lps = log_probs.reshape(1, rows)
    v = pltpu.VMEM
    dma = pltpu.SemaphoreType.DMA
    scratch = [
        v((rows, width), BF16),
        v((4, width, width), BF16),
        v((width, width), BF16),
        v((rows, width), BF16),
        v((rows, width), BF16),
        v((5, rows, width), BF16),
        v((rows, width), F32),
        v((4, rows, width), F32),
        v((rows, width), BF16),
        v((3, rows, width), BF16),
        v((3, rows, width), BF16),
        v((3, rows, width), BF16),
        v((rows, 3 * rows), F32),
        v((rows, 3 * rows), F32),
        v((heads, rows, 3 * rows), F32),
        v((rows, width), F32),
        v((nz, 2 * nx, piece_rows, width), BF16),
        v((nz, 8, rows), F32),
        v((rows, nz * rows), BF16),
        v((rows, width), F32),
        v((rows, width), F32),
        v((2, rows, width), BF16),
        v((2, nx, ny, out_rows, rows), BF16),
        v((nx, ny, out_rows, rows), BF16),
        v((3, rows, width), BF16),
        v((rows, width), F32),
        v((rows, 4 * width), BF16),
        v((rows, width), F32),
        v((rows, width), F32),
        v((rows, width), F32),
        v((2, 2, ny, out_rows, width // 2), BF16),
        v((2, 2, ny, out_rows, width // 2), BF16),
        v((2, ny, out_rows, width // 2), BF16),
        v((2, ny, out_rows, width // 2), BF16),
        v((2, ny, out_rows, width // 2), F32),
        v((ny, out_rows, width), F32),
        v((ny, out_rows, width), BF16),
        v((ny - 1, out_rows, width), BF16),
        v((inner, out_rows, width), BF16),
        v((outer, out_rows, width), BF16),
        dma((9,)),
        dma((4, HALVES)),
        dma((4, HALVES)),
        dma((2, HALVES)),
        dma((2, HALVES)),
        dma((2,)),
        dma((2,)),
        dma((2, 3)),
        dma((2, 3)),
        dma((2,)),
        dma((2,)),
        dma((1,)),
        dma((1,)),
        dma((2,)),
        dma((2,)),
        dma((2, 3)),
        dma((2, 3)),
        dma((1,)),
        dma((1,)),
        dma((inner,)),
        dma((inner,)),
        dma((outer,)),
        dma((outer,)),
    ]
    hbm = pl.BlockSpec(memory_space=pl.ANY)
    vmem = pl.BlockSpec(memory_space=pltpu.VMEM)
    results = pl.pallas_call(
        functools.partial(kernel, (ny, nx, nz, width, heads, events_all)),
        out_shape=(
            jax.ShapeDtypeStruct((rows, width), F32),
            jax.ShapeDtypeStruct((out_rows, width), F32),
        ),
        in_specs=[vmem, vmem, hbm, hbm, hbm, hbm, hbm],
        out_specs=(hbm, vmem),
        scratch_shapes=scratch,
        compiler_params=pltpu.CompilerParams(
            collective_id=0, has_side_effects=True, vmem_limit_bytes=56 * 1024 * 1024
        ),
    )(lens, lps, events, input_weight, output_weight, positives, negatives)
    return pl.pallas_call(
        hand_over,
        out_shape=tuple(jax.ShapeDtypeStruct(r.shape, r.dtype) for r in results),
        in_specs=[vmem, vmem],
        out_specs=(vmem, vmem),
    )(*results)


def solution(mesh):
    sizes = tuple(mesh.shape[a] for a in AXES)
    placed = (
        P(AXES, None),
        P(),
        P(),
        P(AXES, None),
        P("pool", None),
        P("pool"),
        P(),
    )
    return jax.shard_map(
        functools.partial(shards, sizes),
        mesh=mesh,
        in_specs=placed,
        out_specs=(P(AXES, None), P(("dp", "seq"), None)),
        check_vma=False,
    )
```
